512 devices in a mesh: batch: 16 (over z, core), proto: 32 (over x, y).
Axes of the slice: x: 4, y: 8, z: 8, core: 2. Of those that a mesh axis runs over, the one named last changes fastest.
Arguments:
- student_feat: bfloat16 [16384, 256], P('batch', 'proto'), may hold values from -60 to 60
- teacher_feat: bfloat16 [16384, 256], P('batch', 'proto'), may hold values from -60 to 60
- student_proto: bfloat16 [256, 65536], P(None, 'proto'), may hold values from -60 to 60
- teacher_proto: bfloat16 [256, 65536], P(None, 'proto'), may hold values from -60 to 60
Outputs:
- loss_value: float32 [], replicated
- feat_grad: float32 [16384, 256], P('batch', 'proto')
- proto_grad: float32 [256, 65536], P('batch', 'proto')
The draws below stay inside these ranges and needn't reach their ends.
All inputs are finite; a program needn't handle non-finite values.
Results may differ from the reference program's by a relative error of at most 0.0024.
Values may be sent and summed in bfloat16 or wider, within the bound.
No kernel may reach another device: no remote copies, remote signals or barrier semaphores. Data moves between devices by JAX's collectives and lax.ppermute only.
A program may use at most 64 MiB of HBM per device.

```python
import math
import jax
import jax.numpy as jnp
from jax import lax

D = 256
K = 65536
ROWS = 1024
SWEEPS = 3
CROPS = 16384


group_table = (0, 0, 0, 0, 0, 0, 0, 1, 1, 1, 1, 2, 2, 3, 3, 4)


def spread_scales(key, count):
    return jnp.exp(jax.random.uniform(key, (count,), jnp.float32, 0.0, math.log(10.0)))


def crop_labels(key):
    segment_order = jax.random.permutation(jax.random.fold_in(key, 201), 16)
    cluster_order = jax.random.permutation(jax.random.fold_in(key, 202), 8)
    ranks = jnp.array(group_table, jnp.int32)
    segment = jnp.arange(CROPS, dtype=jnp.int32) * 16 // CROPS
    return cluster_order[ranks[segment_order[segment]]]


def column_labels():
    return jnp.arange(K, dtype=jnp.int32) * 8 // K


def centre_table(key, tag):
    return jax.random.normal(jax.random.fold_in(key, tag), (8, D), jnp.float32)


def finish(centred, noise, strength, scales):
    return (jnp.clip(strength * centred + noise, -6.0, 6.0) * scales).astype(jnp.bfloat16)


def draw_student_feat(key, part):
    labels = crop_labels(key)
    centres = centre_table(key, 302)
    key = jax.random.fold_in(key, 11)
    base_key, scale_key = jax.random.split(key, 2)
    scales = spread_scales(scale_key, CROPS)[:, None]
    noise = jax.random.normal(base_key, (CROPS, D), jnp.float32)
    strength = 0.5
    return finish(centres[labels], noise, strength, scales)


def draw_teacher_feat(key, part):
    labels = crop_labels(key)
    centres = centre_table(key, 301)
    key = jax.random.fold_in(key, 12)
    base_key, scale_key = jax.random.split(key, 2)
    scales = spread_scales(scale_key, CROPS)[:, None]
    noise = jax.random.normal(base_key, (CROPS, D), jnp.float32)
    strength = 0.75
    return finish(centres[labels], noise, strength, scales)


def draw_student_proto(key, part):
    centres = centre_table(key, 302)
    key = jax.random.fold_in(key, 13)
    base_key, scale_key = jax.random.split(key, 2)
    scales = spread_scales(scale_key, K)[None, :]
    centred = centres[column_labels()].T
    noise = jax.random.normal(base_key, (D, K), jnp.float32)
    strength = 0.5
    return finish(centred, noise, strength, scales)


def draw_teacher_proto(key, part):
    centres = centre_table(key, 301)
    key = jax.random.fold_in(key, 14)
    base_key, scale_key = jax.random.split(key, 2)
    scales = spread_scales(scale_key, K)[None, :]
    centred = centres[column_labels()].T
    noise = jax.random.normal(base_key, (D, K), jnp.float32)
    strength = 0.75
    return finish(centred, noise, strength, scales)


def setup_inputs(seed: int = 0) -> dict:
    seeds = jax.random.split(jax.random.key(seed), 5)
    return {
        "student_feat": draw_student_feat(jax.random.fold_in(seeds[4], 71), 0),
        "teacher_feat": draw_teacher_feat(jax.random.fold_in(seeds[4], 71), 0),
        "student_proto": draw_student_proto(jax.random.fold_in(seeds[4], 71), 0),
        "teacher_proto": draw_teacher_proto(jax.random.fold_in(seeds[4], 71), 0),
    }


student_temp = 0.1
teacher_temp = 0.07

def unit_rows(raw):
    floated = raw.astype(jnp.float32)
    inverse = lax.rsqrt(lax.optimization_barrier(jnp.sum(floated * floated, axis=1, keepdims=True)) + 1e-06)
    normed = floated * inverse
    return (normed, normed.astype(jnp.bfloat16))

def unit_cols(raw):
    floated = raw.astype(jnp.float32)
    inverse = lax.rsqrt(lax.optimization_barrier(jnp.sum(floated * floated, axis=0, keepdims=True)) + 1e-06)
    normed = floated * inverse
    return (normed, normed.astype(jnp.bfloat16))

def reference(student_feat, teacher_feat, student_proto, teacher_proto):
    feat_unit, feat_round = unit_rows(student_feat)
    teach_normed, teach_round = unit_rows(teacher_feat)
    proto_unit, proto_round = unit_cols(student_proto)
    teach_cols_f, teacher_cols = unit_cols(teacher_proto)
    blocks = CROPS // ROWS

    def teacher_block(block_rows):
        return jnp.exp(jnp.dot(block_rows, teacher_cols, preferred_element_type=jnp.float32) / teacher_temp)
    teacher_exp = lax.map(teacher_block, teach_round.reshape(blocks, ROWS, D)).reshape(CROPS, K)
    row_scale = jnp.ones((CROPS,), jnp.float32)
    col_scale = jnp.ones((K,), jnp.float32)
    for sweep_index in range(SWEEPS):
        column_sum = jnp.dot(row_scale, teacher_exp, precision=lax.Precision.HIGHEST)
        col_scale = 1.0 / (K * column_sum)
        row_sum = jnp.dot(teacher_exp, col_scale, precision=lax.Precision.HIGHEST)
        row_scale = 1.0 / (CROPS * row_sum)

    def student_block(carried, inputs):
        loss_sum, grad_cols = carried
        feat_blk, unit_blk, exp_blk, scale_blk = inputs
        logits = jnp.dot(feat_blk, proto_round, preferred_element_type=jnp.float32) / student_temp
        log_total = jnp.log(lax.optimization_barrier(jnp.sum(jnp.exp(logits), axis=1)))
        target = CROPS * exp_blk * col_scale[None, :] * scale_blk[:, None]
        loss_sum = loss_sum + jnp.sum(log_total) - jnp.sum(target * logits)
        softmax_p = jnp.exp(logits - log_total[:, None])
        grad_logit = (K * (softmax_p - target)).astype(jnp.bfloat16)
        grad_feat = lax.dot_general(grad_logit, proto_round, (((1,), (1,)), ((), ())), preferred_element_type=jnp.float32)
        grad_cols = grad_cols + lax.dot_general(feat_blk, grad_logit, (((0,), (0,)), ((), ())), preferred_element_type=jnp.float32)
        tangent = grad_feat - unit_blk * lax.optimization_barrier(jnp.sum(unit_blk * grad_feat, axis=1, keepdims=True))
        return ((loss_sum, grad_cols), tangent)
    inputs = (feat_round.reshape(blocks, ROWS, D), feat_unit.reshape(blocks, ROWS, D), teacher_exp.reshape(blocks, ROWS, K), row_scale.reshape(blocks, ROWS))
    start = (jnp.zeros((), jnp.float32), jnp.zeros((D, K), jnp.float32))
    (loss_sum, grad_cols), tangents = lax.scan(student_block, start, inputs)
    feat_grad = tangents.reshape(CROPS, D)
    proto_grad = grad_cols - proto_unit * lax.optimization_barrier(jnp.sum(proto_unit * grad_cols, axis=0, keepdims=True))
    return (loss_sum / CROPS, feat_grad, proto_grad)
```

```python
import functools

import jax
import jax.numpy as jnp
from jax import lax
from jax.experimental import pallas as pl
from jax.experimental.pallas import tpu as pltpu
from jax.sharding import PartitionSpec as P

F32, BF16 = jnp.float32, jnp.bfloat16
SWEEPS = 3
LOG2E = 1.4426950408889634
STUDENT_SCALE = LOG2E / 0.1
TEACHER_SCALE = LOG2E / 0.07
D, ROWS, COLS = 256, 1024, 2048
LANES = 128
ROW_TILES, COL_TILES = ROWS // LANES, COLS // LANES
PROTO, BATCH = 32, 16
CROPS, PROTOS = ROWS * BATCH, COLS * PROTO
HALF = ROWS // 2
CHUNK = 512
VMEM_LIMIT = 30 * 1024 * 1024

VM = pl.BlockSpec(memory_space=pltpu.VMEM)
SM = pl.BlockSpec(memory_space=pltpu.SMEM)


def shape(dims, dtype=F32):
    return jax.ShapeDtypeStruct(dims, dtype)


def pinned(dims, dtype=F32):
    return pltpu.VMEM(dims, dtype)


def pin(array):
    return pltpu.with_memory_space_constraint(array, pltpu.VMEM)


def call(body, outs, args, scratch=(), scalars=0, name=None):
    return pl.pallas_call(
        body,
        out_shape=outs,
        in_specs=[SM] * scalars + [VM] * (len(args) - scalars),
        out_specs=[VM] * len(outs),
        scratch_shapes=list(scratch),
        compiler_params=pltpu.CompilerParams(vmem_limit_bytes=VMEM_LIMIT),
        name=name,
    )(*args)


def lane_major(tile):
    return jnp.sum(tile.T, axis=0, keepdims=True)


def sublane_major(row):
    return jnp.broadcast_to(row, (LANES, LANES)).T


def pack_kernel(feat_ref, out_ref):
    x = feat_ref[...].astype(F32)
    both = jnp.concatenate([x[:, :HALF], x[:, HALF:]], axis=0).astype(BF16)
    for peer in range(PROTO):
        out_ref[peer] = both


def unit_cols_kernel(raw_ref, round_ref, inv_ref):
    for lo in range(0, COLS, CHUNK):
        x = raw_ref[:, lo : lo + CHUNK].astype(F32)
        inv = lax.rsqrt(jnp.sum(x * x, axis=0, keepdims=True) + 1e-06)
        inv_ref[:, lo : lo + CHUNK] = inv
        round_ref[:, lo : lo + CHUNK] = (x * inv).astype(BF16)


def unit_rows(feat_ref, half):
    x = feat_ref[:, 8 * half : 8 * half + 8, :].astype(F32).reshape(D, HALF)
    inv = lax.rsqrt(jnp.sum(x * x, axis=0, keepdims=True) + 1e-06)
    return x, inv


def put_cols(out_ref, sums):
    for peer in range(BATCH):
        out_ref[peer] = sums


def put_rows(out_ref, rows, first=0):
    for peer in range(PROTO):
        out_ref[peer, first : first + ROW_TILES, :] = rows


def col_rows(acc_ref):
    total = jnp.sum(acc_ref[...], axis=0, keepdims=True)
    return jnp.concatenate([total[:, LANES * i : LANES * (i + 1)] for i in range(COL_TILES)], axis=0)


def teacher_kernel(feat_ref, cols_ref, exp_ref, out_ref, rows_ref, acc_ref):
    for half in range(2):
        x, inv = unit_rows(feat_ref, half)
        rows_ref[HALF * half : HALF * (half + 1), :] = (x * inv).T.astype(BF16)
    acc_ref[...] = jnp.zeros_like(acc_ref)

    def block(j, carry):
        at = pl.ds(pl.multiple_of(j * LANES, LANES), LANES)
        rows = rows_ref[at, :]
        for lo in range(0, COLS, CHUNK):
            z = jnp.dot(rows, cols_ref[:, lo : lo + CHUNK], preferred_element_type=F32)
            e = jnp.exp2(z * TEACHER_SCALE)
            exp_ref[at, lo : lo + CHUNK] = e
            acc_ref[:, lo : lo + CHUNK] += jnp.sum(e.reshape(LANES // 8, 8, CHUNK), axis=0)
        return carry

    lax.fori_loop(0, ROW_TILES, block, 0)
    put_cols(out_ref, col_rows(acc_ref))


def col_scale_of(got_ref):
    return 1.0 / (PROTOS * jnp.sum(got_ref[...], axis=0))


def row_pass_kernel(exp_ref, got_ref, out_ref, scale_ref, sum_ref):
    scale_ref[...] = col_scale_of(got_ref)

    def block(j, carry):
        at = pl.ds(pl.multiple_of(j * LANES, LANES), LANES)
        acc = jnp.zeros((LANES, LANES), F32)
        for i in range(COL_TILES):
            acc += exp_ref[at, LANES * i : LANES * (i + 1)] * scale_ref[i : i + 1, :]
        sum_ref[pl.ds(j, 1), :] = lane_major(acc)
        return carry

    lax.fori_loop(0, ROW_TILES, block, 0)
    put_rows(out_ref, sum_ref[...])


def col_pass_kernel(exp_ref, got_ref, out_ref, scale_ref, acc_ref):
    scale_ref[...] = 1.0 / (CROPS * jnp.sum(got_ref[...], axis=0))
    acc_ref[...] = jnp.zeros_like(acc_ref)

    def block(j, carry):
        at = pl.ds(pl.multiple_of(j * LANES, LANES), LANES)
        r = sublane_major(scale_ref[pl.ds(j, 1), :])
        for i in range(COL_TILES):
            lanes = slice(LANES * i, LANES * (i + 1))
            acc_ref[:, lanes] += jnp.sum((exp_ref[at, lanes] * r).reshape(LANES // 8, 8, LANES), axis=0)
        return carry

    lax.fori_loop(0, ROW_TILES, block, 0)
    put_cols(out_ref, col_rows(acc_ref))


def student_kernel(feat_ref, cols_ref, rows_ref, feat_out_ref, inv_ref, sum_ref):
    for half in range(2):
        x, inv = unit_rows(feat_ref, half)
        lanes = slice(HALF * half, HALF * (half + 1))
        unit = x * inv
        rows_ref[lanes, :] = unit.T.astype(BF16)
        feat_out_ref[:, lanes] = unit.astype(BF16)
        inv_ref[:, lanes] = inv

    def block(j, carry):
        at = pl.ds(pl.multiple_of(j * LANES, LANES), LANES)
        rows = rows_ref[at, :]
        acc = jnp.zeros((LANES, LANES), F32)
        for lo in range(0, COLS, CHUNK):
            z = jnp.dot(rows, cols_ref[:, lo : lo + CHUNK], preferred_element_type=F32)
            e = jnp.exp2(z * STUDENT_SCALE)
            for i in range(0, CHUNK, LANES):
                acc += e[:, i : i + LANES]
        sum_ref[pl.ds(j, 1), :] = lane_major(acc)
        return carry

    lax.fori_loop(0, ROW_TILES, block, 0)


def last_row_kernel(exp_ref, rows_ref, cols_ref, got_ref, total_ref, out_ref, scale_ref, sum_ref, cross_ref):
    scale_ref[...] = col_scale_of(got_ref)

    def block(j, carry):
        at = pl.ds(pl.multiple_of(j * LANES, LANES), LANES)
        rows = rows_ref[at, :]
        acc = jnp.zeros((LANES, LANES), F32)
        cross = jnp.zeros((LANES, LANES), F32)
        for lo in range(0, COLS, CHUNK):
            z = jnp.dot(rows, cols_ref[:, lo : lo + CHUNK], preferred_element_type=F32)
            for i in range(lo // LANES, (lo + CHUNK) // LANES):
                weighted = exp_ref[at, LANES * i : LANES * (i + 1)] * scale_ref[i : i + 1, :]
                acc += weighted
                cross += weighted * z[:, LANES * i - lo : LANES * (i + 1) - lo]
        sum_ref[pl.ds(j, 1), :] = lane_major(acc)
        cross_ref[pl.ds(j, 1), :] = lane_major(cross)
        return carry

    lax.fori_loop(0, ROW_TILES, block, 0)
    put_rows(out_ref, sum_ref[...])
    put_rows(out_ref, cross_ref[...] / 0.1, ROW_TILES)
    put_rows(out_ref, total_ref[...], 2 * ROW_TILES)


def grad_kernel(
    core_ref, exp_ref, rows_ref, feat_ref, cols_ref, got_ref, scale_ref, raw_feat_ref, feat_inv_ref, raw_cols_ref, cols_inv_ref,
    feat_out_ref, own_ref, other_ref, grad_ref, row_ref, total_ref, col_ref, part_ref,
):
    got = jnp.sum(got_ref[...], axis=0)
    sums, cross, totals = got[:ROW_TILES], got[ROW_TILES : 2 * ROW_TILES], got[2 * ROW_TILES :]
    local_loss = jnp.sum(jnp.log(totals) - cross / sums)
    row_ref[...] = PROTOS / sums
    total_ref[...] = PROTOS / totals
    col_ref[...] = scale_ref[...]

    def block(j, carry):
        at = pl.ds(pl.multiple_of(j * LANES, LANES), LANES)
        rows = rows_ref[at, :]
        target_rows = sublane_major(row_ref[pl.ds(j, 1), :])
        soft_rows = sublane_major(total_ref[pl.ds(j, 1), :])
        for lo in range(0, COLS, CHUNK):
            z = jnp.dot(rows, cols_ref[:, lo : lo + CHUNK], preferred_element_type=F32)
            e = jnp.exp2(z * STUDENT_SCALE)
            for i in range(lo // LANES, (lo + CHUNK) // LANES):
                lanes = slice(LANES * i, LANES * (i + 1))
                target = exp_ref[at, lanes] * col_ref[i : i + 1, :] * target_rows
                soft = e[:, LANES * i - lo : LANES * (i + 1) - lo] * soft_rows
                grad_ref[at, lanes] = (soft - target).astype(BF16)
        return carry

    lax.fori_loop(0, ROW_TILES, block, 0)

    for lo in range(0, COLS, CHUNK):
        lanes = slice(lo, lo + CHUNK)
        part = jnp.dot(feat_ref[...], grad_ref[:, lanes], preferred_element_type=F32)
        unit = raw_cols_ref[:, lanes].astype(F32) * cols_inv_ref[:, lanes]
        part = part - unit * jnp.sum(unit * part, axis=0, keepdims=True)
        part_ref[:, :, :, lanes] = part.reshape(BATCH // 2, 2, D // BATCH, CHUNK)
    core = core_ref[0]
    loss_row = jnp.full((D // BATCH, LANES), local_loss, F32)
    for peer in range(BATCH // 2):
        own_ref[peer, :, :COLS] = part_ref[peer, core]
        other_ref[peer, :, :COLS] = part_ref[peer, 1 - core]
        own_ref[peer, :, COLS:] = loss_row
        other_ref[peer, :, COLS:] = loss_row

    for half in range(2):
        lanes = slice(HALF * half, HALF * (half + 1))
        part = lax.dot_general(
            cols_ref[...], grad_ref[lanes, :], (((1,), (1,)), ((), ())), preferred_element_type=F32
        )
        unit = raw_feat_ref[:, 8 * half : 8 * half + 8, :].astype(F32).reshape(D, HALF) * feat_inv_ref[:, lanes]
        part = part - unit * jnp.sum(unit * part, axis=0, keepdims=True)
        part_ref_half = part.reshape(PROTO, 8, HALF)
        col_part = part_ref_half
        if half == 0:
            first = col_part
    feat_out_ref[...] = jnp.concatenate([first, col_part], axis=1).astype(BF16)


def join_kernel(own_ref, got_ref, out_ref, low_ref):
    total = own_ref[...] + got_ref[...]
    out_ref[:, :, :COLS] = total[:, :, :COLS].astype(BF16)
    tail = total[:, :, COLS:]
    lane = lax.broadcasted_iota(jnp.int32, tail.shape, 2)
    high = tail.astype(BF16).astype(F32)
    middle = (tail - high).astype(BF16).astype(F32)
    low = tail - high - middle
    out_ref[:, :, COLS:] = jnp.where(lane == 0, high, jnp.where(lane == 1, middle, low)).astype(BF16)


def proto_sum_kernel(got_ref, out_ref, loss_ref):
    total = jnp.sum(got_ref[...].astype(F32), axis=0)
    out_ref[...] = total[:, :COLS]
    tail = total[:, COLS:]
    loss_ref[...] = (tail[0:1, 0:1] + tail[0:1, 1:2] + tail[0:1, 2:3]) / CROPS


def feat_sum_kernel(got_ref, out_ref):
    total = jnp.sum(got_ref[...].astype(F32), axis=0)
    out_ref[:, :HALF] = total[:8]
    out_ref[:, HALF:] = total[8:]


def per_device(student_feat, teacher_feat, student_proto, teacher_proto):
    core = lax.rem(lax.axis_index("batch"), 2).astype(jnp.int32).reshape(1)
    swap = [(i, i ^ 1) for i in range(BATCH)]
    z_groups = [list(range(c, BATCH, 2)) for c in range(2)]

    def over_batch(array):
        return lax.all_to_all(array, "batch", 0, 0)

    def over_proto(array):
        return lax.all_to_all(array, "proto", 0, 0)

    packed = shape((PROTO, 16, HALF), BF16)
    row_shape, col_shape = shape((PROTO, ROW_TILES, LANES)), shape((BATCH, COL_TILES, LANES))
    (send_t,) = call(pack_kernel, [packed], [teacher_feat.T], name="pack_teacher")
    (send_s,) = call(pack_kernel, [packed], [student_feat.T], name="pack_student")
    teach = over_proto(send_t)
    stud = over_proto(send_s)
    unit_out = [shape((D, COLS), BF16), shape((1, COLS))]
    teacher_cols, _ = call(unit_cols_kernel, unit_out, [teacher_proto], name="unit_teacher_cols")
    proto_round, proto_inv = call(unit_cols_kernel, unit_out, [student_proto], name="unit_student_cols")

    teacher_exp, send = call(
        teacher_kernel,
        [pinned((ROWS, COLS)), col_shape],
        [teach, teacher_cols],
        [pltpu.VMEM((ROWS, D), BF16), pltpu.VMEM((8, COLS), F32)],
        name="teacher_exp",
    )
    rows_round, feat_round, feat_inv, exp_sum = call(
        student_kernel,
        [shape((ROWS, D), BF16), shape((D, ROWS), BF16), shape((1, ROWS)), shape((ROW_TILES, LANES))],
        [stud, proto_round],
        name="student_exp",
    )
    scale_shape = shape((COL_TILES, LANES))
    for sweep in range(SWEEPS - 1):
        got = over_batch(send)
        send, _ = call(
            row_pass_kernel,
            [row_shape, scale_shape],
            [pin(teacher_exp), got],
            [pltpu.VMEM((ROW_TILES, LANES), F32)],
            name="row_pass",
        )
        got = over_proto(send)
        (send,) = call(
            col_pass_kernel,
            [col_shape],
            [pin(teacher_exp), got],
            [pltpu.VMEM((ROW_TILES, LANES), F32), pltpu.VMEM((8, COLS), F32)],
            name="col_pass",
        )
    got = over_batch(send)
    send, col_scale = call(
        last_row_kernel,
        [shape((PROTO, 3 * ROW_TILES, LANES)), scale_shape],
        [pin(teacher_exp), rows_round, proto_round, got, exp_sum],
        [pltpu.VMEM((ROW_TILES, LANES), F32), pltpu.VMEM((ROW_TILES, LANES), F32)],
        name="last_row_pass",
    )
    got = over_proto(send)
    half_shape = shape((BATCH // 2, D // BATCH, COLS + LANES))
    feat_part, own, other = call(
        grad_kernel,
        [packed, half_shape, half_shape],
        [core, pin(teacher_exp), rows_round, feat_round, proto_round, got, col_scale, stud, feat_inv, student_proto, proto_inv],
        [
            pltpu.VMEM((ROWS, COLS), BF16),
            pltpu.VMEM((ROW_TILES, LANES), F32),
            pltpu.VMEM((ROW_TILES, LANES), F32),
            pltpu.VMEM((COL_TILES, LANES), F32),
            pltpu.VMEM((BATCH // 2, 2, D // BATCH, COLS), F32),
        ],
        scalars=1,
        name="grads",
    )
    arrived = lax.ppermute(other, "batch", swap)
    (joined,) = call(
        functools.partial(join_kernel, low_ref=None),
        [shape((BATCH // 2, D // BATCH, COLS + LANES), BF16)],
        [own, arrived],
        name="join_cores",
    )
    feat_got = over_proto(feat_part)
    proto_got = lax.all_to_all(joined, "batch", 0, 0, axis_index_groups=z_groups)
    (feat_out,) = call(feat_sum_kernel, [shape((8, ROWS))], [feat_got], name="feat_sum")
    proto_out, loss = call(
        proto_sum_kernel, [shape((D // BATCH, COLS)), shape((1, 1))], [proto_got], name="proto_sum"
    )
    return (loss.reshape(()), feat_out.T, proto_out)


def solution(mesh):
    placed = (P("batch", "proto"), P("batch", "proto"), P(None, "proto"), P(None, "proto"))
    return jax.shard_map(
        per_device,
        mesh=mesh,
        in_specs=placed,
        out_specs=(P(), P("batch", "proto"), P("batch", "proto")),
        check_vma=False,
    )
```

```python
import jax
import jax.numpy as jnp
from jax import lax
from jax.experimental import pallas as pl
from jax.experimental.pallas import tpu as pltpu
from jax.sharding import PartitionSpec as P

F32, BF16 = jnp.float32, jnp.bfloat16
SWEEPS = 3
LOG2E = 1.4426950408889634
STUDENT_SCALE = LOG2E / 0.1
TEACHER_SCALE = LOG2E / 0.07
D, ROWS, COLS = 256, 1024, 2048
LANES = 128
ROW_TILES, COL_TILES = ROWS // LANES, COLS // LANES
PROTO, BATCH = 32, 16
PAIRS = BATCH // 4
CROPS, PROTOS = ROWS * BATCH, COLS * PROTO
HALF = ROWS // 2
CHUNK = 512
MIB = 1024 * 1024

VM = pl.BlockSpec(memory_space=pltpu.VMEM)
SM = pl.BlockSpec(memory_space=pltpu.SMEM)
ANY = pl.BlockSpec(memory_space=pl.ANY)


def shape(dims, dtype=F32):
    return jax.ShapeDtypeStruct(dims, dtype)


def pinned(dims, dtype=F32):
    return pltpu.VMEM(dims, dtype)


def pin(array):
    return pltpu.with_memory_space_constraint(array, pltpu.VMEM)


def stay(array):
    return pltpu.with_memory_space_constraint(array, pltpu.HBM)


def call(body, outs, args, scratch=(), specs=None, name=None, vmem=12, aliases=None):
    return pl.pallas_call(
        body,
        out_shape=outs,
        in_specs=specs or [VM] * len(args),
        out_specs=[VM] * len(outs),
        scratch_shapes=list(scratch),
        compiler_params=pltpu.CompilerParams(vmem_limit_bytes=vmem * MIB),
        input_output_aliases=aliases or {},
        name=name,
    )(*args)


def lane_major(partial_ref, out_ref):
    for j in range(ROW_TILES):
        tile = partial_ref[LANES * j : LANES * (j + 1), :]
        out_ref[j : j + 1, :] = jnp.sum(tile.T, axis=0, keepdims=True)


def sublane_major(values, out_ref):
    for j in range(ROW_TILES):
        out_ref[LANES * j : LANES * (j + 1), :] = jnp.broadcast_to(values[j : j + 1, :], (LANES, LANES)).T


def halves(x):
    return jnp.concatenate([x[:, :HALF], x[:, HALF:]], axis=0)


def col_fetches(source_ref, raw_ref, sems):
    lanes = [pl.ds(lo, CHUNK) for lo in range(0, COLS, CHUNK)]
    return [
        pltpu.make_async_copy(source_ref.at[:, here], raw_ref.at[:, here], sems.at[i]) for i, here in enumerate(lanes)
    ]


def unit_cols(fetches, raw_ref, round_ref, inv_ref=None):
    for fetch, lo in zip(fetches, range(0, COLS, CHUNK)):
        fetch.wait()
        x = raw_ref[:, lo : lo + CHUNK].astype(F32)
        inv = lax.rsqrt(jnp.sum(x * x, axis=0, keepdims=True) + 1e-06)
        if inv_ref is not None:
            inv_ref[:, lo : lo + CHUNK] = inv
        round_ref[:, lo : lo + CHUNK] = (x * inv).astype(BF16)


def unit_rows(x):
    return x * lax.rsqrt(jnp.sum(x * x, axis=0, keepdims=True) + 1e-06)


def prepare_kernel(place_ref, teach_ref, stud_ref, teach_out, stud_out, place_out):
    both = halves(teach_ref[...].astype(F32)).astype(BF16)
    for peer in range(PROTO):
        teach_out[peer] = both
    stud_out[...] = stud_ref[...].astype(F32)
    place_out[0] = place_ref[0]


def put(out_ref, value, rows=slice(None), lanes=slice(None)):
    for peer in range(out_ref.shape[0]):
        out_ref[peer, rows, lanes] = value


def col_rows(acc_ref):
    total = jnp.sum(acc_ref[...], axis=0, keepdims=True)
    return jnp.concatenate([total[:, LANES * i : LANES * (i + 1)] for i in range(COL_TILES)], axis=0)


def row_block(j):
    return pl.ds(pl.multiple_of(j * LANES, LANES), LANES)


def teacher_kernel(feat_ref, source_ref, exp_ref, out_ref, rows_ref, raw_cols_ref, cols_ref, acc_ref, sems):
    fetches = col_fetches(source_ref, raw_cols_ref, sems)
    for fetch in fetches:
        fetch.start()
    for half in range(2):
        x = feat_ref[:, 8 * half : 8 * half + 8, :].astype(F32).reshape(D, HALF)
        rows_ref[HALF * half : HALF * (half + 1), :] = unit_rows(x).T.astype(BF16)
    unit_cols(fetches, raw_cols_ref, cols_ref)
    acc_ref[...] = jnp.zeros_like(acc_ref)

    def block(j, carry):
        at = row_block(j)
        rows = rows_ref[at, :]
        for lo in range(0, COLS, CHUNK):
            z = jnp.dot(rows, cols_ref[:, lo : lo + CHUNK], preferred_element_type=F32)
            e = jnp.exp2(z * TEACHER_SCALE)
            exp_ref[at, lo : lo + CHUNK] = e
            acc_ref[:, lo : lo + CHUNK] += jnp.sum(e.reshape(LANES // 8, 8, CHUNK), axis=0)
        return carry

    lax.fori_loop(0, ROW_TILES, block, 0)
    put(out_ref, col_rows(acc_ref).astype(out_ref.dtype))


def col_scale_of(got_ref):
    return 1.0 / (PROTOS * jnp.sum(got_ref[...].astype(F32), axis=0))


def row_sums(exp_ref, scale_ref, part_ref, sum_ref):
    def block(j, carry):
        at = row_block(j)
        acc = jnp.zeros((LANES, LANES), F32)
        for i in range(COL_TILES):
            acc += exp_ref[at, LANES * i : LANES * (i + 1)] * scale_ref[i : i + 1, :]
        part_ref[at, :] = acc
        return carry

    lax.fori_loop(0, ROW_TILES, block, 0)
    lane_major(part_ref, sum_ref)


def row_kernel(exp_ref, got_ref, out_ref, scale_ref, part_ref, sum_ref):
    scale_ref[...] = col_scale_of(got_ref)
    row_sums(exp_ref, scale_ref, part_ref, sum_ref)
    put(out_ref, sum_ref[...])


def col_kernel(exp_ref, got_ref, out_ref, rows_ref, acc_ref):
    sublane_major(1.0 / (CROPS * jnp.sum(got_ref[...], axis=0)), rows_ref)
    acc_ref[...] = jnp.zeros_like(acc_ref)

    def block(j, carry):
        at = row_block(j)
        r = rows_ref[at, :]
        for i in range(COL_TILES):
            lanes = slice(LANES * i, LANES * (i + 1))
            acc_ref[:, lanes] += jnp.sum((exp_ref[at, lanes] * r).reshape(LANES // 8, 8, LANES), axis=0)
        return carry

    lax.fori_loop(0, ROW_TILES, block, 0)
    put(out_ref, col_rows(acc_ref).astype(out_ref.dtype))


def student_kernel(
    gathered_ref, source_ref, send_ref, exp_ref, rows_ref, raw_feat_ref, feat_out_ref, feat_inv_ref, raw_cols_ref, cols_ref,
    cols_inv_ref, sum_ref, out_ref, part_ref, feat_ref, sems, sem,
):
    fetches = col_fetches(source_ref, raw_cols_ref, sems)
    for fetch in fetches:
        fetch.start()
    fetch = pltpu.make_async_copy(gathered_ref, feat_ref, sem)
    fetch.start()
    out_ref[...] = send_ref[...]
    unit_cols(fetches, raw_cols_ref, cols_ref, cols_inv_ref)
    fetch.wait()
    for half in range(2):
        lanes = slice(HALF * half, HALF * (half + 1))
        x = feat_ref[:, lanes]
        raw_feat_ref[:, lanes] = x.astype(BF16)
        inv = lax.rsqrt(jnp.sum(x * x, axis=0, keepdims=True) + 1e-06)
        unit = x * inv
        rows_ref[lanes, :] = unit.T.astype(BF16)
        feat_out_ref[:, lanes] = unit.astype(BF16)
        feat_inv_ref[:, lanes] = inv

    def block(j, carry):
        at = row_block(j)
        rows = rows_ref[at, :]
        acc = jnp.zeros((LANES, LANES), F32)
        for lo in range(0, COLS, CHUNK):
            z = jnp.dot(rows, cols_ref[:, lo : lo + CHUNK], preferred_element_type=F32)
            e = jnp.exp2(z * STUDENT_SCALE)
            exp_ref[at, lo : lo + CHUNK] = e
            for i in range(0, CHUNK, LANES):
                acc += e[:, i : i + LANES]
        part_ref[at, :] = acc
        return carry

    lax.fori_loop(0, ROW_TILES, block, 0)
    lane_major(part_ref, sum_ref)


def last_row_kernel(
    source_ref, rows_ref, cols_ref, got_ref, total_ref, out_ref, weighted_ref, scale_ref, part_ref, cross_ref, sum_ref, sems
):
    def fetch(j):
        at = row_block(j)
        return pltpu.make_async_copy(source_ref.at[at, :], weighted_ref.at[at, :], sems.at[j])

    for j in range(ROW_TILES):
        fetch(j).start()
    scale_ref[...] = col_scale_of(got_ref)

    def block(j, carry):
        at = row_block(j)
        rows = rows_ref[at, :]
        acc = jnp.zeros((LANES, LANES), F32)
        cross = jnp.zeros((LANES, LANES), F32)
        fetch(j).wait()
        for lo in range(0, COLS, CHUNK):
            z = jnp.dot(rows, cols_ref[:, lo : lo + CHUNK], preferred_element_type=F32)
            for i in range(lo // LANES, (lo + CHUNK) // LANES):
                lanes = slice(LANES * i, LANES * (i + 1))
                weighted = weighted_ref[at, lanes] * scale_ref[i : i + 1, :]
                weighted_ref[at, lanes] = weighted
                acc += weighted
                cross += weighted * z[:, LANES * i - lo : LANES * (i + 1) - lo]
        part_ref[at, :] = acc
        cross_ref[at, :] = cross
        return carry

    lax.fori_loop(0, ROW_TILES, block, 0)
    lane_major(part_ref, sum_ref)
    put(out_ref, sum_ref[...], rows=slice(0, ROW_TILES))
    lane_major(cross_ref, sum_ref)
    put(out_ref, sum_ref[...] / 0.1, rows=slice(ROW_TILES, 2 * ROW_TILES))
    put(out_ref, total_ref[...], rows=slice(2 * ROW_TILES, 3 * ROW_TILES))


def grad_kernel(
    place_ref, weighted_ref, exp_ref, feat_ref, got_ref, raw_cols_ref, cols_inv_ref,
    grad_ref, own_ref, other_ref, target_ref, soft_ref, part_ref,
):
    got = jnp.sum(got_ref[...], axis=0)
    sums, cross, totals = got[:ROW_TILES], got[ROW_TILES : 2 * ROW_TILES], got[2 * ROW_TILES :]
    local_loss = jnp.sum(jnp.log(totals) - cross / sums)
    sublane_major(PROTOS / sums, target_ref)
    sublane_major(PROTOS / totals, soft_ref)

    def block(j, carry):
        at = row_block(j)
        target_rows, soft_rows = target_ref[at, :], soft_ref[at, :]
        for i in range(COL_TILES):
            lanes = slice(LANES * i, LANES * (i + 1))
            grad_ref[at, lanes] = (exp_ref[at, lanes] * soft_rows - weighted_ref[at, lanes] * target_rows).astype(BF16)
        return carry

    lax.fori_loop(0, ROW_TILES, block, 0)

    for lo in range(0, COLS, CHUNK):
        lanes = slice(lo, lo + CHUNK)
        part = jnp.dot(feat_ref[...], grad_ref[:, lanes], preferred_element_type=F32)
        unit = raw_cols_ref[:, lanes].astype(F32) * cols_inv_ref[:, lanes]
        part = part - unit * jnp.sum(unit * part, axis=0, keepdims=True)
        part_ref[:, :, :, :, lanes] = part.reshape(PAIRS, 2, 2, D // BATCH, CHUNK)
    core, odd = lax.rem(place_ref[0], 2), lax.rem(lax.div(place_ref[0], 2), 2)
    loss_row = jnp.full((D // BATCH, LANES), local_loss, F32)
    for away in range(2):
        parity = odd if away == 0 else 1 - odd
        for pair in range(PAIRS):
            own_ref[away, pair, :, :COLS] = part_ref[pair, parity, core]
            other_ref[away, pair, :, :COLS] = part_ref[pair, parity, 1 - core]
            own_ref[away, pair, :, COLS:] = loss_row
            other_ref[away, pair, :, COLS:] = loss_row


def feat_grad_kernel(grad_ref, cols_ref, raw_feat_ref, feat_inv_ref, out_ref):
    parts = []
    for half in range(2):
        lanes = slice(HALF * half, HALF * (half + 1))
        part = lax.dot_general(
            cols_ref[...], grad_ref[lanes, :], (((1,), (1,)), ((), ())), preferred_element_type=F32
        )
        unit = raw_feat_ref[:, lanes].astype(F32) * feat_inv_ref[:, lanes]
        part = part - unit * jnp.sum(unit * part, axis=0, keepdims=True)
        parts.append(part.reshape(PROTO, 8, HALF))
    out_ref[...] = jnp.concatenate(parts, axis=1).astype(BF16)


def join_cores_kernel(own_ref, got_ref, feat_ref, keep_ref, send_ref, feat_out_ref):
    keep_ref[...] = own_ref[0] + got_ref[0]
    send_ref[...] = own_ref[1] + got_ref[1]


def join_pairs_kernel(own_ref, got_ref, after_ref, out_ref):
    total = own_ref[...] + got_ref[...]
    out_ref[:, :, :COLS] = total[:, :, :COLS].astype(BF16)
    tail = total[:, :, COLS:]
    lane = lax.broadcasted_iota(jnp.int32, tail.shape, 2)
    high = tail.astype(BF16).astype(F32)
    middle = (tail - high).astype(BF16).astype(F32)
    low = tail - high - middle
    out_ref[:, :, COLS:] = jnp.where(lane == 0, high, jnp.where(lane == 1, middle, low)).astype(BF16)


def final_kernel(feat_ref, proto_ref, feat_out_ref, proto_out_ref, loss_ref):
    total = jnp.sum(proto_ref[...].astype(F32), axis=0)
    proto_out_ref[...] = total[:, :COLS]
    tail = total[:, COLS:]
    loss_ref[...] = (tail[0:1, 0:1] + tail[0:1, 1:2] + tail[0:1, 2:3]) / CROPS
    feat = jnp.sum(feat_ref[...].astype(F32), axis=0)
    feat_out_ref[:, :HALF] = feat[:8]
    feat_out_ref[:, HALF:] = feat[8:]


def per_device(student_feat, teacher_feat, student_proto, teacher_proto):
    place = lax.axis_index("batch").astype(jnp.int32).reshape(1)
    swap_cores = [(i, i ^ 1) for i in range(BATCH)]
    swap_pairs = [(i, i ^ 2) for i in range(BATCH)]
    quads = [list(range(first, BATCH, 4)) for first in range(4)]

    def over_batch(array):
        return lax.all_to_all(array, "batch", 0, 0)

    def over_proto(array):
        return lax.all_to_all(array, "proto", 0, 0)

    packed = shape((PROTO, 16, HALF), BF16)
    rounded = shape((D, COLS), BF16)
    rounded_rows = shape((ROWS, D), BF16)
    row_shape = shape((PROTO, ROW_TILES, LANES))
    last_shape = shape((PROTO, 3 * ROW_TILES, LANES))
    col_shape, last_col_shape = shape((BATCH, COL_TILES, LANES), BF16), shape((BATCH, COL_TILES, LANES))
    row_tile, row_part = pltpu.VMEM((ROW_TILES, LANES), F32), pltpu.VMEM((ROWS, LANES), F32)
    col_tile, col_part = pltpu.VMEM((COL_TILES, LANES), F32), pltpu.VMEM((8, COLS), F32)

    send, stud_send, place = pl.pallas_call(
        prepare_kernel,
        out_shape=[packed, shape((8, ROWS)), shape((1,), jnp.int32)],
        in_specs=[SM, VM, VM],
        out_specs=[VM, VM, SM],
        name="prepare",
    )(place, teacher_feat.T, student_feat.T)
    stud = lax.all_gather(stud_send, "proto", axis=0, tiled=True)
    teach = over_proto(send)
    teacher_exp, send = call(
        teacher_kernel,
        [pinned((ROWS, COLS)), col_shape],
        [teach, stay(teacher_proto)],
        [
            pltpu.VMEM((ROWS, D), BF16),
            pltpu.VMEM((D, COLS), BF16),
            pltpu.VMEM((D, COLS), BF16),
            col_part,
            pltpu.SemaphoreType.DMA((COLS // CHUNK,)),
        ],
        specs=[VM, ANY],
        name="teacher_exp",
    )
    for sweep in range(SWEEPS - 1):
        got = over_batch(send)
        (send,) = call(
            row_kernel, [row_shape], [pin(teacher_exp), got], [col_tile, row_part, row_tile], name="row_pass"
        )
        got = over_proto(send)
        (send,) = call(
            col_kernel,
            [col_shape if sweep + 2 < SWEEPS else last_col_shape],
            [pin(teacher_exp), got],
            [row_part, col_part],
            name="col_pass",
        )
    student_exp, rows_round, raw_feat, feat_round, feat_inv, raw_proto, proto_round, proto_inv, exp_sum, send = call(
        student_kernel,
        [
            pinned((ROWS, COLS)),
            rounded_rows,
            shape((D, ROWS), BF16),
            shape((D, ROWS), BF16),
            shape((1, ROWS)),
            rounded,
            rounded,
            shape((1, COLS)),
            shape((ROW_TILES, LANES)),
            last_col_shape,
        ],
        [stay(stud), stay(student_proto), send],
        [
            row_part,
            pltpu.VMEM((D, ROWS), F32),
            pltpu.SemaphoreType.DMA((COLS // CHUNK,)),
            pltpu.SemaphoreType.DMA,
        ],
        specs=[ANY, ANY, VM],
        name="student_exp",
    )
    got = over_batch(send)
    send, weighted = call(
        last_row_kernel,
        [last_shape, pinned((ROWS, COLS))],
        [stay(teacher_exp), rows_round, proto_round, got, exp_sum],
        [col_tile, row_part, row_part, row_tile, pltpu.SemaphoreType.DMA((ROW_TILES,))],
        specs=[ANY] + [VM] * 4,
        name="last_row_pass",
    )
    got = over_proto(send)
    half_shape = shape((2, PAIRS, D // BATCH, COLS + LANES))
    grad_logit, own, other = call(
        grad_kernel,
        [pinned((ROWS, COLS), BF16), half_shape, half_shape],
        [place, pin(weighted), pin(student_exp), feat_round, got, raw_proto, proto_inv],
        [row_part, row_part, pltpu.VMEM((PAIRS, 2, 2, D // BATCH, COLS), F32)],
        specs=[SM] + [VM] * 6,
        vmem=16,
        name="proto_grad",
    )
    arrived = lax.ppermute(other, "batch", swap_cores)
    (feat_part,) = call(
        feat_grad_kernel, [packed], [pin(grad_logit), proto_round, raw_feat, feat_inv], name="feat_grad"
    )
    pair_shape = (PAIRS, D // BATCH, COLS + LANES)
    keep, send, feat_part = pl.pallas_call(
        join_cores_kernel,
        out_shape=[shape(pair_shape), shape(pair_shape), packed],
        in_specs=[VM, VM, ANY],
        out_specs=[VM, VM, ANY],
        input_output_aliases={2: 2},
        compiler_params=pltpu.CompilerParams(vmem_limit_bytes=12 * MIB),
        name="join_cores",
    )(own, arrived, feat_part)
    feat_got = over_proto(feat_part)
    arrived = lax.ppermute(send, "batch", swap_pairs)
    (joined,) = call(join_pairs_kernel, [shape(pair_shape, BF16)], [keep, arrived, feat_got], specs=[VM, VM, ANY], name="join_pairs")
    proto_got = lax.all_to_all(joined, "batch", 0, 0, axis_index_groups=quads)
    feat_out, proto_out, loss = call(
        final_kernel,
        [shape((8, ROWS)), shape((D // BATCH, COLS)), shape((1, 1))],
        [feat_got, proto_got],
        name="final_sums",
    )
    return (loss.reshape(()), feat_out.T, proto_out)


def solution(mesh):
    placed = (P("batch", "proto"), P("batch", "proto"), P(None, "proto"), P(None, "proto"))
    return jax.shard_map(
        per_device,
        mesh=mesh,
        in_specs=placed,
        out_specs=(P(), P("batch", "proto"), P("batch", "proto")),
        check_vma=False,
    )
```

```python
import jax
import jax.numpy as jnp
from jax import lax
from jax.experimental import pallas as pl
from jax.experimental.pallas import tpu as pltpu
from jax.sharding import PartitionSpec as P

F32, BF16 = jnp.float32, jnp.bfloat16
SWEEPS = 3
LOG2E = 1.4426950408889634
STUDENT_SCALE = LOG2E / 0.1
TEACHER_SCALE = LOG2E / 0.07
D, ROWS, COLS = 256, 1024, 2048
LANES = 128
ROW_TILES, COL_TILES = ROWS // LANES, COLS // LANES
PROTO, BATCH = 32, 16
PAIRS = BATCH // 4
CROPS, PROTOS = ROWS * BATCH, COLS * PROTO
HALF = ROWS // 2
CHUNK = 512
MIB = 1024 * 1024

VM = pl.BlockSpec(memory_space=pltpu.VMEM)
SM = pl.BlockSpec(memory_space=pltpu.SMEM)
ANY = pl.BlockSpec(memory_space=pl.ANY)


def shape(dims, dtype=F32):
    return jax.ShapeDtypeStruct(dims, dtype)


def pinned(dims, dtype=F32):
    return pltpu.VMEM(dims, dtype)


def pin(array):
    return pltpu.with_memory_space_constraint(array, pltpu.VMEM)


def stay(array):
    return pltpu.with_memory_space_constraint(array, pltpu.HBM)


def call(body, outs, args, scratch=(), specs=None, name=None, vmem=12, aliases=None):
    return pl.pallas_call(
        body,
        out_shape=outs,
        in_specs=specs or [VM] * len(args),
        out_specs=[VM] * len(outs),
        scratch_shapes=list(scratch),
        compiler_params=pltpu.CompilerParams(vmem_limit_bytes=vmem * MIB),
        input_output_aliases=aliases or {},
        name=name,
    )(*args)


def lane_major(partial_ref, out_ref):
    for j in range(ROW_TILES):
        tile = partial_ref[LANES * j : LANES * (j + 1), :]
        out_ref[j : j + 1, :] = jnp.sum(tile.T, axis=0, keepdims=True)


def sublane_major(values, out_ref):
    for j in range(ROW_TILES):
        out_ref[LANES * j : LANES * (j + 1), :] = jnp.broadcast_to(values[j : j + 1, :], (LANES, LANES)).T


def prepare_kernel(place_ref, teach_ref, stud_ref, teach_out, stud_out, place_out):
    place_out[0] = place_ref[0]
    stud_out[...] = stud_ref[...].astype(F32)
    put(teach_out, teach_ref[...])


def unit_cols_kernel(teacher_ref, student_ref, teacher_out, student_out, inv_ref):
    for lo in range(0, COLS, CHUNK):
        lanes = slice(lo, lo + CHUNK)
        teacher_out[:, lanes] = unit_rows(teacher_ref[:, lanes].astype(F32)).astype(BF16)
        x = student_ref[:, lanes].astype(F32)
        inv = lax.rsqrt(jnp.sum(x * x, axis=0, keepdims=True) + 1e-06)
        inv_ref[:, lanes] = inv
        student_out[:, lanes] = (x * inv).astype(BF16)


def unit_rows(x):
    return x * lax.rsqrt(jnp.sum(x * x, axis=0, keepdims=True) + 1e-06)


def put(out_ref, value, rows=slice(None), lanes=slice(None)):
    for peer in range(out_ref.shape[0]):
        out_ref[peer, rows, lanes] = value


def col_rows(acc_ref):
    total = jnp.sum(acc_ref[...], axis=0, keepdims=True)
    return jnp.concatenate([total[:, LANES * i : LANES * (i + 1)] for i in range(COL_TILES)], axis=0)


def row_block(j):
    return pl.ds(pl.multiple_of(j * LANES, LANES), LANES)


def teacher_kernel(feat_ref, cols_ref, exp_ref, out_ref, rows_ref, acc_ref):
    for half in range(2):
        lanes = slice(HALF * half, HALF * (half + 1))
        x = feat_ref[:, :, lanes].astype(F32).reshape(D, HALF)
        rows_ref[lanes, :] = unit_rows(x).T.astype(BF16)
    acc_ref[...] = jnp.zeros_like(acc_ref)

    def block(j, carry):
        at = row_block(j)
        rows = rows_ref[at, :]
        for lo in range(0, COLS, CHUNK):
            z = jnp.dot(rows, cols_ref[:, lo : lo + CHUNK], preferred_element_type=F32)
            e = jnp.exp2(z * TEACHER_SCALE)
            exp_ref[at, lo : lo + CHUNK] = e
            acc_ref[:, lo : lo + CHUNK] += jnp.sum(e.reshape(LANES // 8, 8, CHUNK), axis=0)
        return carry

    lax.fori_loop(0, ROW_TILES, block, 0)
    put(out_ref, col_rows(acc_ref).astype(out_ref.dtype))


def col_scale_of(got_ref):
    return 1.0 / (PROTOS * jnp.sum(got_ref[...].astype(F32), axis=0))


def row_sums(exp_ref, scale_ref, part_ref, sum_ref):
    def block(j, carry):
        at = row_block(j)
        acc = jnp.zeros((LANES, LANES), F32)
        for i in range(COL_TILES):
            acc += exp_ref[at, LANES * i : LANES * (i + 1)] * scale_ref[i : i + 1, :]
        part_ref[at, :] = acc
        return carry

    lax.fori_loop(0, ROW_TILES, block, 0)
    lane_major(part_ref, sum_ref)


def row_kernel(exp_ref, got_ref, out_ref, scale_ref, part_ref, sum_ref):
    scale_ref[...] = col_scale_of(got_ref)
    row_sums(exp_ref, scale_ref, part_ref, sum_ref)
    put(out_ref, sum_ref[...].astype(out_ref.dtype))


def col_kernel(exp_ref, got_ref, out_ref, rows_ref, acc_ref):
    sublane_major(1.0 / (CROPS * jnp.sum(got_ref[...].astype(F32), axis=0)), rows_ref)
    acc_ref[...] = jnp.zeros_like(acc_ref)

    def block(j, carry):
        at = row_block(j)
        r = rows_ref[at, :]
        for i in range(COL_TILES):
            lanes = slice(LANES * i, LANES * (i + 1))
            acc_ref[:, lanes] += jnp.sum((exp_ref[at, lanes] * r).reshape(LANES // 8, 8, LANES), axis=0)
        return carry

    lax.fori_loop(0, ROW_TILES, block, 0)
    put(out_ref, col_rows(acc_ref).astype(out_ref.dtype))


def student_kernel(
    gathered_ref, source_ref, cols_ref, got_ref, exp_ref, weighted_ref, raw_feat_ref, feat_out_ref, feat_inv_ref, out_ref,
    feat_ref, teacher_ref, rows_ref, scale_ref, part_ref, cross_ref, total_ref, sum_ref, feat_sems, sems,
):
    def feat_fetch(half):
        lanes = pl.ds(HALF * half, HALF)
        return pltpu.make_async_copy(gathered_ref.at[:, lanes], feat_ref.at[half], feat_sems.at[half])

    def fetch(j):
        at = row_block(j)
        return pltpu.make_async_copy(source_ref.at[at, :], teacher_ref.at[at, :], sems.at[j])

    for half in range(2):
        feat_fetch(half).start()
    for j in range(ROW_TILES):
        fetch(j).start()
    scale_ref[...] = col_scale_of(got_ref)
    for half in range(2):
        lanes = slice(HALF * half, HALF * (half + 1))
        feat_fetch(half).wait()
        x = feat_ref[half]
        raw_feat_ref[:, lanes] = x.astype(BF16)
        inv = lax.rsqrt(jnp.sum(x * x, axis=0, keepdims=True) + 1e-06)
        unit = x * inv
        rows_ref[lanes, :] = unit.T.astype(BF16)
        feat_out_ref[:, lanes] = unit.astype(BF16)
        feat_inv_ref[:, lanes] = inv

    def block(j, carry):
        at = row_block(j)
        rows = rows_ref[at, :]
        acc = jnp.zeros((LANES, LANES), F32)
        cross = jnp.zeros((LANES, LANES), F32)
        total = jnp.zeros((LANES, LANES), F32)
        fetch(j).wait()
        for lo in range(0, COLS, CHUNK):
            z = jnp.dot(rows, cols_ref[:, lo : lo + CHUNK], preferred_element_type=F32)
            e = jnp.exp2(z * STUDENT_SCALE)
            exp_ref[at, lo : lo + CHUNK] = e
            for i in range(lo // LANES, (lo + CHUNK) // LANES):
                lanes = slice(LANES * i, LANES * (i + 1))
                here = slice(LANES * i - lo, LANES * (i + 1) - lo)
                weighted = teacher_ref[at, lanes] * scale_ref[i : i + 1, :]
                weighted_ref[at, lanes] = weighted
                acc += weighted
                cross += weighted * z[:, here]
                total += e[:, here]
        part_ref[at, :] = acc
        cross_ref[at, :] = cross
        total_ref[at, :] = total
        return carry

    lax.fori_loop(0, ROW_TILES, block, 0)
    sends = []
    for ref in (part_ref, total_ref, cross_ref):
        lane_major(ref, sum_ref)
        high = sum_ref[...].astype(BF16).astype(F32)
        sends += [high, sum_ref[...] - high]
    put(out_ref, jnp.concatenate(sends[:5], axis=0).astype(BF16))


def grad_kernel(
    place_ref, weighted_ref, exp_ref, feat_ref, got_ref, source_ref, cols_inv_ref,
    grad_ref, own_ref, other_ref, target_ref, soft_ref, order_ref, raw_cols_ref, sems,
):
    core, odd = lax.rem(place_ref[0], 2), lax.rem(lax.div(place_ref[0], 2), 2)
    fetches = []
    for away in range(2):
        parity = odd if away == 0 else 1 - odd
        for side in range(2):
            other = core if side == 0 else 1 - core
            fetches.append(
                pltpu.make_async_copy(source_ref.at[:, parity, other], raw_cols_ref.at[side, away], sems.at[len(fetches)])
            )
            for pair in range(PAIRS):
                order_ref[side, away, pair] = feat_ref[pair, parity, other]
    for fetch in fetches:
        fetch.start()
    got = jnp.sum(got_ref[...].astype(F32), axis=0).reshape(5, ROW_TILES, LANES)
    sums, totals, cross = got[0] + got[1], got[2] + got[3], got[4] / 0.1
    local_loss = jnp.sum(jnp.log(totals) - cross / sums)
    sublane_major(PROTOS / sums, target_ref)
    sublane_major(PROTOS / totals, soft_ref)

    def block(j, carry):
        at = row_block(j)
        target_rows, soft_rows = target_ref[at, :], soft_ref[at, :]
        for i in range(COL_TILES):
            lanes = slice(LANES * i, LANES * (i + 1))
            grad_ref[at, lanes] = (exp_ref[at, lanes] * soft_rows - weighted_ref[at, lanes] * target_rows).astype(BF16)
        return carry

    lax.fori_loop(0, ROW_TILES, block, 0)

    for fetch in fetches:
        fetch.wait()
    half_block = (2, PAIRS, D // BATCH, CHUNK)
    for lo in range(0, COLS, CHUNK):
        lanes = slice(lo, lo + CHUNK)
        rows = order_ref[...].reshape(D, ROWS)
        part = jnp.dot(rows, grad_ref[:, lanes], preferred_element_type=F32)
        unit = raw_cols_ref[:, :, :, :, lanes].astype(F32).reshape(D, CHUNK) * cols_inv_ref[:, lanes]
        part = part - unit * jnp.sum(unit * part, axis=0, keepdims=True)
        own_ref[:, :, :, lanes] = part[: D // 2].reshape(half_block)
        other_ref[:, :, :, lanes] = part[D // 2 :].reshape(half_block)
    loss_row = jnp.full((2, PAIRS, D // BATCH, LANES), local_loss, F32)
    own_ref[:, :, :, COLS:] = loss_row
    other_ref[:, :, :, COLS:] = loss_row


def feat_grad_kernel(grad_ref, cols_ref, raw_feat_ref, feat_inv_ref, out_ref):
    for half in range(2):
        lanes = slice(HALF * half, HALF * (half + 1))
        part = lax.dot_general(
            cols_ref[...], grad_ref[lanes, :], (((1,), (1,)), ((), ())), preferred_element_type=F32
        )
        unit = raw_feat_ref[:, lanes].astype(F32) * feat_inv_ref[:, lanes]
        part = part - unit * jnp.sum(unit * part, axis=0, keepdims=True)
        out_ref[:, :, lanes] = part.reshape(PROTO, 8, HALF).astype(BF16)


def join_cores_kernel(own_ref, got_ref, feat_ref, keep_ref, send_ref, feat_out_ref):
    keep_ref[...] = own_ref[0] + got_ref[0]
    send_ref[...] = own_ref[1] + got_ref[1]


def join_pairs_kernel(own_ref, got_ref, after_ref, out_ref):
    total = own_ref[...] + got_ref[...]
    out_ref[:, :, :COLS] = total[:, :, :COLS].astype(BF16)
    tail = total[:, :, COLS:]
    lane = lax.broadcasted_iota(jnp.int32, tail.shape, 2)
    high = tail.astype(BF16).astype(F32)
    middle = (tail - high).astype(BF16).astype(F32)
    low = tail - high - middle
    out_ref[:, :, COLS:] = jnp.where(lane == 0, high, jnp.where(lane == 1, middle, low)).astype(BF16)


def final_kernel(feat_ref, proto_ref, feat_out_ref, proto_out_ref, loss_ref):
    total = jnp.sum(proto_ref[...].astype(F32), axis=0)
    proto_out_ref[...] = total[:, :COLS]
    tail = total[:, COLS:]
    loss_ref[...] = (tail[0:1, 0:1] + tail[0:1, 1:2] + tail[0:1, 2:3]) / CROPS
    feat_out_ref[...] = jnp.sum(feat_ref[...].astype(F32), axis=0)


def per_device(student_feat, teacher_feat, student_proto, teacher_proto):
    place = lax.axis_index("batch").astype(jnp.int32).reshape(1)
    swap_cores = [(i, i ^ 1) for i in range(BATCH)]
    swap_pairs = [(i, i ^ 2) for i in range(BATCH)]
    quads = [list(range(first, BATCH, 4)) for first in range(4)]

    def over_batch(array):
        return lax.all_to_all(array, "batch", 0, 0)

    def over_proto(array):
        return lax.all_to_all(array, "proto", 0, 0)

    packed = shape((PROTO, 8, ROWS), BF16)
    rounded = shape((D, COLS), BF16)
    row_shape = shape((PROTO, ROW_TILES, LANES), BF16)
    last_shape = shape((PROTO, 5 * ROW_TILES, LANES), BF16)
    col_shape, last_col_shape = shape((BATCH, COL_TILES, LANES), BF16), shape((BATCH, COL_TILES, LANES))
    row_tile, row_part = pltpu.VMEM((ROW_TILES, LANES), F32), pltpu.VMEM((ROWS, LANES), F32)
    col_tile, col_part = pltpu.VMEM((COL_TILES, LANES), F32), pltpu.VMEM((8, COLS), F32)

    send, stud_send, place = pl.pallas_call(
        prepare_kernel,
        out_shape=[packed, shape((8, ROWS)), shape((1,), jnp.int32)],
        in_specs=[SM, VM, VM],
        out_specs=[VM, VM, SM],
        name="prepare",
    )(place, teacher_feat.T, student_feat.T)
    stud = lax.all_gather(stud_send, "proto", axis=0, tiled=True)
    teach = over_proto(send)
    teacher_cols, proto_round, proto_inv = call(
        unit_cols_kernel, [rounded, rounded, shape((1, COLS))], [teacher_proto, student_proto], name="unit_cols"
    )
    teacher_exp, send = call(
        teacher_kernel,
        [pinned((ROWS, COLS)), col_shape],
        [teach, teacher_cols],
        [pltpu.VMEM((ROWS, D), BF16), col_part],
        name="teacher_exp",
    )
    for sweep in range(SWEEPS - 1):
        got = over_batch(send)
        (send,) = call(
            row_kernel, [row_shape], [pin(teacher_exp), got], [col_tile, row_part, row_tile], name="row_pass"
        )
        got = over_proto(send)
        (send,) = call(
            col_kernel,
            [col_shape if sweep + 2 < SWEEPS else last_col_shape],
            [pin(teacher_exp), got],
            [row_part, col_part],
            name="col_pass",
        )
    got = over_batch(send)
    student_exp, weighted, raw_feat, feat_round, feat_inv, send = call(
        student_kernel,
        [
            pinned((ROWS, COLS)),
            pinned((ROWS, COLS)),
            shape((D, ROWS), BF16),
            shape((D, ROWS), BF16),
            shape((1, ROWS)),
            last_shape,
        ],
        [stay(stud), stay(teacher_exp), proto_round, got],
        [
            pltpu.VMEM((2, D, HALF), F32),
            pltpu.VMEM((ROWS, COLS), F32),
            pltpu.VMEM((ROWS, D), BF16),
            col_tile,
            row_part,
            row_part,
            row_part,
            row_tile,
            pltpu.SemaphoreType.DMA((2,)),
            pltpu.SemaphoreType.DMA((ROW_TILES,)),
        ],
        specs=[ANY, ANY, VM, VM],
        vmem=20,
        name="student_and_last_row",
    )
    got = over_proto(send)
    half_shape = shape((2, PAIRS, D // BATCH, COLS + LANES))
    split = (PAIRS, 2, 2, D // BATCH)
    order = (2, 2, PAIRS, D // BATCH)
    grad_logit, own, other = call(
        grad_kernel,
        [pinned((ROWS, COLS), BF16), half_shape, half_shape],
        [
            place,
            pin(weighted),
            pin(student_exp),
            feat_round.reshape(split + (ROWS,)),
            got,
            stay(student_proto.reshape(split + (COLS,))),
            proto_inv,
        ],
        [
            row_part,
            row_part,
            pltpu.VMEM(order + (ROWS,), BF16),
            pltpu.VMEM(order + (COLS,), BF16),
            pltpu.SemaphoreType.DMA((4,)),
        ],
        specs=[SM] + [VM] * 4 + [ANY, VM],
        vmem=16,
        name="proto_grad",
    )
    arrived = lax.ppermute(other, "batch", swap_cores)
    (feat_part,) = call(
        feat_grad_kernel, [packed], [pin(grad_logit), proto_round, raw_feat, feat_inv], name="feat_grad"
    )
    pair_shape = (PAIRS, D // BATCH, COLS + LANES)
    keep, send, feat_part = pl.pallas_call(
        join_cores_kernel,
        out_shape=[shape(pair_shape), shape(pair_shape), packed],
        in_specs=[VM, VM, ANY],
        out_specs=[VM, VM, ANY],
        input_output_aliases={2: 2},
        compiler_params=pltpu.CompilerParams(vmem_limit_bytes=12 * MIB),
        name="join_cores",
    )(own, arrived, feat_part)
    feat_got = over_proto(feat_part)
    arrived = lax.ppermute(send, "batch", swap_pairs)
    (joined,) = call(join_pairs_kernel, [shape(pair_shape, BF16)], [keep, arrived, feat_got], specs=[VM, VM, ANY], name="join_pairs")
    proto_got = lax.all_to_all(joined, "batch", 0, 0, axis_index_groups=quads)
    feat_out, proto_out, loss = call(
        final_kernel,
        [shape((8, ROWS)), shape((D // BATCH, COLS)), shape((1, 1))],
        [feat_got, proto_got],
        name="final_sums",
    )
    return (loss.reshape(()), feat_out.T, proto_out)


def solution(mesh):
    placed = (P("batch", "proto"), P("batch", "proto"), P(None, "proto"), P(None, "proto"))
    return jax.shard_map(
        per_device,
        mesh=mesh,
        in_specs=placed,
        out_specs=(P(), P("batch", "proto"), P("batch", "proto")),
        check_vma=False,
    )
```

```python
import jax
import jax.numpy as jnp
from jax import lax
from jax.experimental import pallas as pl
from jax.experimental.pallas import tpu as pltpu
from jax.sharding import PartitionSpec as P

F32, BF16 = jnp.float32, jnp.bfloat16
SWEEPS = 3
LOG2E = 1.4426950408889634
STUDENT_SCALE = LOG2E / 0.1
TEACHER_SCALE = LOG2E / 0.07
D, ROWS, COLS = 256, 1024, 2048
LANES = 128
ROW_TILES, COL_TILES = ROWS // LANES, COLS // LANES
PROTO, BATCH = 32, 16
PAIRS = BATCH // 4
SIDE = 8
CROPS, PROTOS = ROWS * BATCH, COLS * PROTO
HALF = ROWS // 2
CHUNK = 512
BAND = 32
MIB = 1024 * 1024

VM = pl.BlockSpec(memory_space=pltpu.VMEM)
SM = pl.BlockSpec(memory_space=pltpu.SMEM)
ANY = pl.BlockSpec(memory_space=pl.ANY)


def shape(dims, dtype=F32):
    return jax.ShapeDtypeStruct(dims, dtype)


def pinned(dims, dtype=F32):
    return pltpu.VMEM(dims, dtype)


def pin(array):
    return pltpu.with_memory_space_constraint(array, pltpu.VMEM)


def stay(array):
    return pltpu.with_memory_space_constraint(array, pltpu.HBM)


def call(body, outs, args, scratch=(), specs=None, name=None, vmem=12, aliases=None):
    return pl.pallas_call(
        body,
        out_shape=outs,
        in_specs=specs or [VM] * len(args),
        out_specs=[VM] * len(outs),
        scratch_shapes=list(scratch),
        compiler_params=pltpu.CompilerParams(vmem_limit_bytes=vmem * MIB),
        input_output_aliases=aliases or {},
        name=name,
    )(*args)


def lane_major(partial_ref, out_ref):
    for j in range(ROW_TILES):
        tile = partial_ref[LANES * j : LANES * (j + 1), :]
        out_ref[j : j + 1, :] = jnp.sum(tile.T, axis=0, keepdims=True)


def sublane_major(values, out_ref):
    for j in range(ROW_TILES):
        out_ref[LANES * j : LANES * (j + 1), :] = jnp.broadcast_to(values[j : j + 1, :], (LANES, LANES)).T


def prepare_kernel(place_ref, teach_ref, teach_out, place_out):
    place_out[0] = place_ref[0]
    put(teach_out, teach_ref[...])


def unit_cols_kernel(teacher_ref, student_ref, teacher_out, student_out, inv_ref):
    for lo in range(0, COLS, CHUNK):
        lanes = slice(lo, lo + CHUNK)
        teacher_out[:, lanes] = unit_rows(teacher_ref[:, lanes].astype(F32)).astype(BF16)
        x = student_ref[:, lanes].astype(F32)
        inv = lax.rsqrt(jnp.sum(x * x, axis=0, keepdims=True) + 1e-06)
        inv_ref[:, lanes] = inv
        student_out[:, lanes] = (x * inv).astype(BF16)


def unit_rows(x):
    return x * lax.rsqrt(jnp.sum(x * x, axis=0, keepdims=True) + 1e-06)


def put(out_ref, value, rows=slice(None), lanes=slice(None)):
    for peer in range(out_ref.shape[0]):
        out_ref[peer, rows, lanes] = value


def col_rows(acc_ref):
    total = jnp.sum(acc_ref[...], axis=0, keepdims=True)
    return jnp.concatenate([total[:, LANES * i : LANES * (i + 1)] for i in range(COL_TILES)], axis=0)


def row_block(j):
    return pl.ds(pl.multiple_of(j * LANES, LANES), LANES)


def teacher_kernel(feat_ref, cols_ref, exp_ref, out_ref, rows_ref, acc_ref):
    for half in range(2):
        lanes = slice(HALF * half, HALF * (half + 1))
        x = feat_ref[:, :, lanes].astype(F32).reshape(D, HALF)
        rows_ref[lanes, :] = unit_rows(x).T.astype(BF16)
    for lo in range(0, COLS, CHUNK):
        lanes = slice(lo, lo + CHUNK)
        z = jnp.dot(rows_ref[...], cols_ref[:, lanes], preferred_element_type=F32)
        e = jnp.exp2(z * TEACHER_SCALE)
        exp_ref[:, lanes] = e
        acc_ref[:, lanes] = jnp.sum(e.reshape(ROWS // 8, 8, CHUNK), axis=0)
    put(out_ref, col_rows(acc_ref).astype(out_ref.dtype))


def col_scale_of(got_ref):
    return 1.0 / (PROTOS * jnp.sum(got_ref[...].astype(F32), axis=0))


def row_sums(exp_ref, scale_ref, part_ref, sum_ref):
    def block(pair, carry):
        for j in (2 * pair, 2 * pair + 1):
            at = row_block(j)
            acc = jnp.zeros((LANES, LANES), F32)
            for i in range(COL_TILES):
                acc += exp_ref[at, LANES * i : LANES * (i + 1)] * scale_ref[i : i + 1, :]
            part_ref[at, :] = acc
        return carry

    lax.fori_loop(0, ROW_TILES // 2, block, 0)
    lane_major(part_ref, sum_ref)


def first_row_kernel(exp_ref, got_ref, stud_ref, out_ref, scale_ref, part_ref, sum_ref):
    scale_ref[...] = col_scale_of(got_ref)
    row_sums(exp_ref, scale_ref, part_ref, sum_ref)
    sums = sum_ref[...].astype(BF16)
    for peer in range(PROTO):
        half = peer // SIDE % 2
        out_ref[peer, :, :HALF] = stud_ref[:, HALF * half : HALF * (half + 1)]
        out_ref[peer, :, HALF:] = sums


def row_kernel(exp_ref, got_ref, after_ref, out_ref, scale_ref, part_ref, sum_ref):
    scale_ref[...] = col_scale_of(got_ref)
    row_sums(exp_ref, scale_ref, part_ref, sum_ref)
    put(out_ref, sum_ref[...].astype(BF16))


def col_kernel(exp_ref, got_ref, out_ref, rows_ref, acc_ref):
    sublane_major(1.0 / (CROPS * jnp.sum(got_ref[:, :, -LANES:].astype(F32), axis=0)), rows_ref)
    acc_ref[...] = jnp.zeros_like(acc_ref)

    def block(j, carry):
        at = row_block(j)
        r = rows_ref[at, :]
        for i in range(COL_TILES):
            lanes = slice(LANES * i, LANES * (i + 1))
            acc_ref[:, lanes] += jnp.sum((exp_ref[at, lanes] * r).reshape(LANES // 8, 8, LANES), axis=0)
        return carry

    lax.fori_loop(0, ROW_TILES, block, 0)
    put(out_ref, col_rows(acc_ref).astype(out_ref.dtype))


def student_kernel(
    place_ref, own_ref, other_ref, teacher_ref, cols_ref, got_ref, exp_ref, weighted_ref, raw_feat_ref, feat_out_ref, feat_inv_ref,
    out_ref, rows_ref, scale_ref, part_ref, cross_ref, total_ref, sum_ref,
):
    scale_ref[...] = col_scale_of(got_ref)
    side = lax.rem(lax.div(place_ref[0], SIDE), 2)
    for half in range(2):
        lanes = slice(HALF * half, HALF * (half + 1))
        own, other = own_ref[:, :, :HALF].astype(F32), other_ref[:, :, :HALF].astype(F32)
        x = jnp.where(side == half, own, other).reshape(D, HALF)
        raw_feat_ref[:, lanes] = x.astype(BF16)
        inv = lax.rsqrt(jnp.sum(x * x, axis=0, keepdims=True) + 1e-06)
        unit = x * inv
        rows_ref[lanes, :] = unit.T.astype(BF16)
        feat_out_ref[:, lanes] = unit.astype(BF16)
        feat_inv_ref[:, lanes] = inv

    for lo in range(0, COLS, CHUNK):
        z = jnp.dot(rows_ref[...], cols_ref[:, lo : lo + CHUNK], preferred_element_type=F32)
        for top in range(0, ROWS, BAND):
            band = slice(top, top + BAND)
            if lo == 0:
                acc = cross = total = jnp.zeros((BAND, LANES), F32)
            else:
                acc, cross, total = part_ref[band, :], cross_ref[band, :], total_ref[band, :]
            for i in range(lo // LANES, (lo + CHUNK) // LANES):
                lanes = slice(LANES * i, LANES * (i + 1))
                logit = z[band, LANES * i - lo : LANES * (i + 1) - lo]
                e = jnp.exp2(logit * STUDENT_SCALE)
                exp_ref[band, lanes] = e
                weighted = teacher_ref[band, lanes] * scale_ref[i : i + 1, :]
                weighted_ref[band, lanes] = weighted
                acc += weighted
                cross += weighted * logit
                total += e
            part_ref[band, :], cross_ref[band, :], total_ref[band, :] = acc, cross, total
    sends = []
    for ref in (part_ref, total_ref, cross_ref):
        lane_major(ref, sum_ref)
        high = sum_ref[...].astype(BF16).astype(F32)
        sends += [high, sum_ref[...] - high]
    put(out_ref, jnp.concatenate(sends[:5], axis=0).astype(BF16))


def grad_kernel(
    place_ref, weighted_ref, exp_ref, feat_ref, got_ref, source_ref, cols_inv_ref,
    grad_ref, own_ref, other_ref, target_ref, soft_ref, order_ref, raw_cols_ref, sems,
):
    batch = lax.div(place_ref[0], PROTO)
    core, odd = lax.rem(batch, 2), lax.rem(lax.div(batch, 2), 2)
    fetches = []
    for away in range(2):
        parity = odd if away == 0 else 1 - odd
        for side in range(2):
            other = core if side == 0 else 1 - core
            fetches.append(
                pltpu.make_async_copy(source_ref.at[:, parity, other], raw_cols_ref.at[side, away], sems.at[len(fetches)])
            )
            for pair in range(PAIRS):
                order_ref[side, away, pair] = feat_ref[pair, parity, other]
    for fetch in fetches:
        fetch.start()
    got = jnp.sum(got_ref[...].astype(F32), axis=0).reshape(5, ROW_TILES, LANES)
    sums, totals, cross = got[0] + got[1], got[2] + got[3], got[4] / 0.1
    local_loss = jnp.sum(jnp.log(totals) - cross / sums)
    sublane_major(PROTOS / sums, target_ref)
    sublane_major(PROTOS / totals, soft_ref)

    def block(j, carry):
        at = pl.ds(pl.multiple_of(j * 64, 64), 64)
        target_rows, soft_rows = target_ref[at, :], soft_ref[at, :]
        for i in range(COL_TILES):
            lanes = slice(LANES * i, LANES * (i + 1))
            grad_ref[at, lanes] = (exp_ref[at, lanes] * soft_rows - weighted_ref[at, lanes] * target_rows).astype(BF16)
        return carry

    lax.fori_loop(0, ROWS // 64, block, 0)

    for fetch in fetches:
        fetch.wait()
    half_block = (2, PAIRS, D // BATCH, CHUNK)
    for lo in range(0, COLS, CHUNK):
        lanes = slice(lo, lo + CHUNK)
        rows = order_ref[...].reshape(D, ROWS)
        part = jnp.dot(rows, grad_ref[:, lanes], preferred_element_type=F32)
        unit = raw_cols_ref[:, :, :, :, lanes].astype(F32).reshape(D, CHUNK) * cols_inv_ref[:, lanes]
        part = part - unit * jnp.sum(unit * part, axis=0, keepdims=True)
        own_ref[:, :, :, lanes] = part[: D // 2].reshape(half_block)
        other_ref[:, :, :, lanes] = part[D // 2 :].reshape(half_block)
    loss_row = jnp.full((2, PAIRS, D // BATCH, LANES), local_loss, F32)
    own_ref[:, :, :, COLS:] = loss_row
    other_ref[:, :, :, COLS:] = loss_row


def feat_grad_kernel(grad_ref, cols_ref, raw_feat_ref, feat_inv_ref, out_ref):
    for half in range(2):
        lanes = slice(HALF * half, HALF * (half + 1))
        part = lax.dot_general(
            cols_ref[...], grad_ref[lanes, :], (((1,), (1,)), ((), ())), preferred_element_type=F32
        )
        unit = raw_feat_ref[:, lanes].astype(F32) * feat_inv_ref[:, lanes]
        part = part - unit * jnp.sum(unit * part, axis=0, keepdims=True)
        out_ref[:, :, lanes] = part.reshape(PROTO, 8, HALF).astype(BF16)


def spread(tail):
    lane = lax.broadcasted_iota(jnp.int32, tail.shape, 2)
    high = tail.astype(BF16).astype(F32)
    middle = (tail - high).astype(BF16).astype(F32)
    return jnp.where(lane == 0, high, jnp.where(lane == 1, middle, tail - high - middle)).astype(BF16)


def gather_parts(tail):
    return tail[..., 0:1] + tail[..., 1:2] + tail[..., 2:3]


def join_cores_kernel(own_ref, got_ref, feat_ref, keep_ref, send_ref, feat_out_ref):
    keep_ref[...] = own_ref[0] + got_ref[0]
    away = own_ref[1] + got_ref[1]
    send_ref[:, :, :COLS] = away[:, :, :COLS].astype(BF16)
    send_ref[:, :, COLS:] = spread(away[:, :, COLS:])


def join_pairs_kernel(own_ref, got_ref, after_ref, out_ref):
    got = got_ref[...].astype(F32)
    out_ref[:, :, :COLS] = (own_ref[:, :, :COLS] + got[:, :, :COLS]).astype(BF16)
    out_ref[:, :, COLS:] = spread(own_ref[:, :, COLS:] + gather_parts(got[:, :, COLS:]))


def final_kernel(feat_ref, proto_ref, feat_out_ref, proto_out_ref, loss_ref):
    total = jnp.sum(proto_ref[...].astype(F32), axis=0)
    proto_out_ref[...] = total[:, :COLS]
    loss_ref[...] = gather_parts(total[0:1, COLS:]) / CROPS
    feat_out_ref[...] = jnp.sum(feat_ref[...].astype(F32), axis=0)


def per_device(student_feat, teacher_feat, student_proto, teacher_proto):
    place = (lax.axis_index("batch") * PROTO + lax.axis_index("proto")).astype(jnp.int32).reshape(1)
    swap_cores = [(i, i ^ 1) for i in range(BATCH)]
    swap_pairs = [(i, i ^ 2) for i in range(BATCH)]
    swap_sides = [(i, i ^ SIDE) for i in range(PROTO)]
    quads = [list(range(first, BATCH, 4)) for first in range(4)]

    def over_batch(array):
        return lax.all_to_all(array, "batch", 0, 0)

    def over_proto(array):
        return lax.all_to_all(array, "proto", 0, 0)

    packed = shape((PROTO, 8, ROWS), BF16)
    rounded = shape((D, COLS), BF16)
    row_shape = shape((PROTO, ROW_TILES, LANES), BF16)
    first_row_shape = shape((PROTO, ROW_TILES, HALF + LANES), BF16)
    last_shape = shape((PROTO, 5 * ROW_TILES, LANES), BF16)
    col_shape, last_col_shape = shape((BATCH, COL_TILES, LANES), BF16), shape((BATCH, COL_TILES, LANES))
    row_tile, row_part = pltpu.VMEM((ROW_TILES, LANES), F32), pltpu.VMEM((ROWS, LANES), F32)
    col_tile, col_part = pltpu.VMEM((COL_TILES, LANES), F32), pltpu.VMEM((8, COLS), F32)

    send, place = pl.pallas_call(
        prepare_kernel,
        out_shape=[packed, shape((1,), jnp.int32)],
        in_specs=[SM, VM],
        out_specs=[VM, SM],
        name="prepare",
    )(place, teacher_feat.T)
    teach = over_proto(send)
    teacher_cols, proto_round, proto_inv = call(
        unit_cols_kernel, [rounded, rounded, shape((1, COLS))], [teacher_proto, student_proto], name="unit_cols"
    )
    teacher_exp, send = call(
        teacher_kernel,
        [pinned((ROWS, COLS)), col_shape],
        [teach, teacher_cols],
        [pltpu.VMEM((ROWS, D), BF16), col_part],
        name="teacher_exp",
    )
    got = over_batch(send)
    (send,) = call(
        first_row_kernel,
        [first_row_shape],
        [pin(teacher_exp), got, student_feat.T],
        [col_tile, row_part, row_tile],
        name="row_pass_1",
    )
    own_half = over_proto(send)
    other_half = lax.ppermute(own_half, "proto", swap_sides)
    (send,) = call(
        col_kernel, [col_shape], [pin(teacher_exp), own_half], [row_part, col_part], name="col_pass_2"
    )
    got = over_batch(send)
    (send,) = call(
        row_kernel,
        [row_shape],
        [pin(teacher_exp), got, other_half],
        [col_tile, row_part, row_tile],
        specs=[VM, VM, ANY],
        name="row_pass_2",
    )
    got = over_proto(send)
    (send,) = call(col_kernel, [last_col_shape], [pin(teacher_exp), got], [row_part, col_part], name="col_pass_3")
    got = over_batch(send)
    student_exp, weighted, raw_feat, feat_round, feat_inv, send = call(
        student_kernel,
        [
            pinned((ROWS, COLS)),
            pinned((ROWS, COLS)),
            shape((D, ROWS), BF16),
            shape((D, ROWS), BF16),
            shape((1, ROWS)),
            last_shape,
        ],
        [place, own_half, other_half, pin(teacher_exp), proto_round, got],
        [pltpu.VMEM((ROWS, D), BF16), col_tile, row_part, row_part, row_part, row_tile],
        specs=[SM] + [VM] * 5,
        name="student_and_last_row",
    )
    got = over_proto(send)
    half_shape = shape((2, PAIRS, D // BATCH, COLS + LANES))
    split = (PAIRS, 2, 2, D // BATCH)
    order = (2, 2, PAIRS, D // BATCH)
    grad_logit, own, other = call(
        grad_kernel,
        [pinned((ROWS, COLS), BF16), half_shape, half_shape],
        [
            place,
            pin(weighted),
            pin(student_exp),
            feat_round.reshape(split + (ROWS,)),
            got,
            stay(student_proto.reshape(split + (COLS,))),
            proto_inv,
        ],
        [
            row_part,
            row_part,
            pltpu.VMEM(order + (ROWS,), BF16),
            pltpu.VMEM(order + (COLS,), BF16),
            pltpu.SemaphoreType.DMA((4,)),
        ],
        specs=[SM] + [VM] * 4 + [ANY, VM],
        vmem=16,
        name="proto_grad",
    )
    arrived = lax.ppermute(other, "batch", swap_cores)
    (feat_part,) = call(
        feat_grad_kernel, [packed], [pin(grad_logit), proto_round, raw_feat, feat_inv], name="feat_grad"
    )
    pair_shape = (PAIRS, D // BATCH, COLS + LANES)
    keep, send, feat_part = pl.pallas_call(
        join_cores_kernel,
        out_shape=[shape(pair_shape), shape(pair_shape, BF16), packed],
        in_specs=[VM, VM, ANY],
        out_specs=[VM, VM, ANY],
        input_output_aliases={2: 2},
        compiler_params=pltpu.CompilerParams(vmem_limit_bytes=12 * MIB),
        name="join_cores",
    )(own, arrived, feat_part)
    feat_got = over_proto(feat_part)
    arrived = lax.ppermute(send, "batch", swap_pairs)
    (joined,) = call(join_pairs_kernel, [shape(pair_shape, BF16)], [keep, arrived, feat_got], specs=[VM, VM, ANY], name="join_pairs")
    proto_got = lax.all_to_all(joined, "batch", 0, 0, axis_index_groups=quads)
    feat_out, proto_out, loss = call(
        final_kernel,
        [shape((8, ROWS)), shape((D // BATCH, COLS)), shape((1, 1))],
        [feat_got, proto_got],
        name="final_sums",
    )
    return (loss.reshape(()), feat_out.T, proto_out)


def solution(mesh):
    placed = (P("batch", "proto"), P("batch", "proto"), P(None, "proto"), P(None, "proto"))
    return jax.shard_map(
        per_device,
        mesh=mesh,
        in_specs=placed,
        out_specs=(P(), P("batch", "proto"), P("batch", "proto")),
        check_vma=False,
    )
```

```python
import jax
import jax.numpy as jnp
from jax import lax
from jax.experimental import pallas as pl
from jax.experimental.pallas import tpu as pltpu
from jax.sharding import PartitionSpec as P

F32, BF16 = jnp.float32, jnp.bfloat16
SWEEPS = 3
LOG2E = 1.4426950408889634
STUDENT_SCALE = LOG2E / 0.1
TEACHER_SCALE = LOG2E / 0.07
D, ROWS, COLS = 256, 1024, 2048
LANES = 128
ROW_TILES, COL_TILES = ROWS // LANES, COLS // LANES
PROTO, BATCH = 32, 16
PAIRS = BATCH // 4
SIDE = 8
CROPS, PROTOS = ROWS * BATCH, COLS * PROTO
HALF = ROWS // 2
QUARTER = ROWS // 4
CHUNK = 512
BAND = 32
MIB = 1024 * 1024
LONG = 200_000_000_000

VM = pl.BlockSpec(memory_space=pltpu.VMEM)
SM = pl.BlockSpec(memory_space=pltpu.SMEM)
ANY = pl.BlockSpec(memory_space=pl.ANY)


def shape(dims, dtype=F32):
    return jax.ShapeDtypeStruct(dims, dtype)


def pinned(dims, dtype=F32):
    return pltpu.VMEM(dims, dtype)


def pin(array):
    return pltpu.with_memory_space_constraint(array, pltpu.VMEM)


def stay(array):
    return pltpu.with_memory_space_constraint(array, pltpu.HBM)


def call(body, outs, args, scratch=(), specs=None, name=None, vmem=12, aliases=None, flops=None):
    return pl.pallas_call(
        body,
        out_shape=outs,
        in_specs=specs or [VM] * len(args),
        out_specs=[VM] * len(outs),
        scratch_shapes=list(scratch),
        compiler_params=pltpu.CompilerParams(vmem_limit_bytes=vmem * MIB),
        input_output_aliases=aliases or {},
        cost_estimate=flops and pl.CostEstimate(flops=flops, bytes_accessed=0, transcendentals=0),
        name=name,
    )(*args)


def lane_major(partial_ref, out_ref):
    for j in range(ROW_TILES):
        tile = partial_ref[LANES * j : LANES * (j + 1), :]
        out_ref[j : j + 1, :] = jnp.sum(tile.T, axis=0, keepdims=True)


def sublane_major(values, out_ref):
    for j in range(ROW_TILES):
        out_ref[LANES * j : LANES * (j + 1), :] = jnp.broadcast_to(values[j : j + 1, :], (LANES, LANES)).T


def prepare_kernel(place_ref, teach_ref, teach_out, place_out):
    place_out[0] = place_ref[0]
    put(teach_out, teach_ref[...])


def unit_cols_kernel(teacher_ref, student_ref, teacher_out, student_out, inv_ref):
    for lo in range(0, COLS, CHUNK):
        lanes = slice(lo, lo + CHUNK)
        teacher_out[:, lanes] = unit_rows(teacher_ref[:, lanes].astype(F32)).astype(BF16)
        x = student_ref[:, lanes].astype(F32)
        inv = lax.rsqrt(jnp.sum(x * x, axis=0, keepdims=True) + 1e-06)
        inv_ref[:, lanes] = inv
        student_out[:, lanes] = (x * inv).astype(BF16)


def unit_rows(x):
    return x * lax.rsqrt(jnp.sum(x * x, axis=0, keepdims=True) + 1e-06)


def put(out_ref, value, rows=slice(None), lanes=slice(None)):
    for peer in range(out_ref.shape[0]):
        out_ref[peer, rows, lanes] = value


def col_rows(acc_ref):
    total = jnp.sum(acc_ref[...], axis=0, keepdims=True)
    return jnp.concatenate([total[:, LANES * i : LANES * (i + 1)] for i in range(COL_TILES)], axis=0)


def row_block(j):
    return pl.ds(pl.multiple_of(j * LANES, LANES), LANES)


def teacher_kernel(feat_ref, cols_ref, exp_ref, out_ref, rows_ref, acc_ref):
    for half in range(2):
        lanes = slice(HALF * half, HALF * (half + 1))
        x = feat_ref[:, :, lanes].astype(F32).reshape(D, HALF)
        rows_ref[lanes, :] = unit_rows(x).T.astype(BF16)
    for lo in range(0, COLS, CHUNK):
        lanes = slice(lo, lo + CHUNK)
        z = jnp.dot(rows_ref[...], cols_ref[:, lanes], preferred_element_type=F32)
        e = jnp.exp2(z * TEACHER_SCALE)
        exp_ref[:, lanes] = e
        acc_ref[:, lanes] = jnp.sum(e.reshape(ROWS // 8, 8, CHUNK), axis=0)
    put(out_ref, col_rows(acc_ref).astype(out_ref.dtype))


def col_scale_of(got_ref):
    return 1.0 / (PROTOS * jnp.sum(got_ref[...].astype(F32), axis=0))


def row_sums(exp_ref, scale_ref, part_ref, sum_ref):
    def block(pair, carry):
        for j in (2 * pair, 2 * pair + 1):
            at = row_block(j)
            acc = jnp.zeros((LANES, LANES), F32)
            for i in range(COL_TILES):
                acc += exp_ref[at, LANES * i : LANES * (i + 1)] * scale_ref[i : i + 1, :]
            part_ref[at, :] = acc
        return carry

    lax.fori_loop(0, ROW_TILES // 2, block, 0)
    lane_major(part_ref, sum_ref)


def first_row_kernel(exp_ref, got_ref, stud_ref, out_ref, scale_ref, part_ref, sum_ref):
    scale_ref[...] = col_scale_of(got_ref)
    row_sums(exp_ref, scale_ref, part_ref, sum_ref)
    sums = sum_ref[...].astype(BF16)
    for peer in range(PROTO):
        half = peer // SIDE % 2
        out_ref[peer, :, :HALF] = stud_ref[:, HALF * half : HALF * (half + 1)]
        out_ref[peer, :, HALF:] = sums


def row_kernel(exp_ref, got_ref, after_ref, out_ref, scale_ref, part_ref, sum_ref):
    scale_ref[...] = col_scale_of(got_ref)
    row_sums(exp_ref, scale_ref, part_ref, sum_ref)
    put(out_ref, sum_ref[...].astype(BF16))


def col_kernel(exp_ref, got_ref, out_ref, rows_ref, acc_ref):
    sublane_major(1.0 / (CROPS * jnp.sum(got_ref[:, :, -LANES:].astype(F32), axis=0)), rows_ref)
    acc_ref[...] = jnp.zeros_like(acc_ref)

    def block(j, carry):
        at = row_block(j)
        r = rows_ref[at, :]
        for i in range(COL_TILES):
            lanes = slice(LANES * i, LANES * (i + 1))
            acc_ref[:, lanes] += jnp.sum((exp_ref[at, lanes] * r).reshape(LANES // 8, 8, LANES), axis=0)
        return carry

    lax.fori_loop(0, ROW_TILES, block, 0)
    put(out_ref, col_rows(acc_ref).astype(out_ref.dtype))


def student_kernel(
    place_ref, own_ref, other_ref, teacher_ref, cols_ref, got_ref, exp_ref, weighted_ref, raw_feat_ref, feat_out_ref, feat_inv_ref,
    out_ref, rows_ref, scale_ref, part_ref, cross_ref, total_ref, sum_ref,
):
    scale_ref[...] = col_scale_of(got_ref)
    side = lax.rem(lax.div(place_ref[0], SIDE), 2)
    for half in range(2):
        lanes = slice(HALF * half, HALF * (half + 1))
        own, other = own_ref[:, :, :HALF].astype(F32), other_ref[:, :, :HALF].astype(F32)
        x = jnp.where(side == half, own, other).reshape(D, HALF)
        raw_feat_ref[:, lanes] = x.astype(BF16)
        inv = lax.rsqrt(jnp.sum(x * x, axis=0, keepdims=True) + 1e-06)
        unit = x * inv
        rows_ref[lanes, :] = unit.T.astype(BF16)
        feat_out_ref[:, lanes] = unit.astype(BF16)
        feat_inv_ref[:, lanes] = inv

    for lo in range(0, COLS, CHUNK):
        z = jnp.dot(rows_ref[...], cols_ref[:, lo : lo + CHUNK], preferred_element_type=F32)
        for top in range(0, ROWS, BAND):
            band = slice(top, top + BAND)
            if lo == 0:
                acc = cross = total = jnp.zeros((BAND, LANES), F32)
            else:
                acc, cross, total = part_ref[band, :], cross_ref[band, :], total_ref[band, :]
            for i in range(lo // LANES, (lo + CHUNK) // LANES):
                lanes = slice(LANES * i, LANES * (i + 1))
                logit = z[band, LANES * i - lo : LANES * (i + 1) - lo]
                e = jnp.exp2(logit * STUDENT_SCALE)
                exp_ref[band, lanes] = e
                weighted = teacher_ref[band, lanes] * scale_ref[i : i + 1, :]
                weighted_ref[band, lanes] = weighted
                acc += weighted
                cross += weighted * logit
                total += e
            part_ref[band, :], cross_ref[band, :], total_ref[band, :] = acc, cross, total
    sends = []
    for ref in (part_ref, total_ref, cross_ref):
        lane_major(ref, sum_ref)
        high = sum_ref[...].astype(BF16).astype(F32)
        sends += [high, sum_ref[...] - high]
    put(out_ref, jnp.concatenate(sends[:5], axis=0).astype(BF16))


def grad_kernel(
    place_ref, weighted_ref, exp_ref, feat_ref, got_ref, source_ref, cols_inv_ref,
    grad_ref, own_ref, other_ref, target_ref, soft_ref, order_ref, raw_cols_ref, sems,
):
    batch = lax.div(place_ref[0], PROTO)
    core, odd = lax.rem(batch, 2), lax.rem(lax.div(batch, 2), 2)
    fetches = []
    for away in range(2):
        parity = odd if away == 0 else 1 - odd
        for side in range(2):
            other = core if side == 0 else 1 - core
            fetches.append(
                pltpu.make_async_copy(source_ref.at[:, parity, other], raw_cols_ref.at[side, away], sems.at[len(fetches)])
            )
            for pair in range(PAIRS):
                order_ref[side, away, pair] = feat_ref[pair, parity, other]
    for fetch in fetches:
        fetch.start()
    got = jnp.sum(got_ref[...].astype(F32), axis=0).reshape(5, ROW_TILES, LANES)
    sums, totals, cross = got[0] + got[1], got[2] + got[3], got[4] / 0.1
    local_loss = jnp.sum(jnp.log(totals) - cross / sums)
    sublane_major(PROTOS / sums, target_ref)
    sublane_major(PROTOS / totals, soft_ref)

    def block(j, carry):
        at = pl.ds(pl.multiple_of(j * 64, 64), 64)
        target_rows, soft_rows = target_ref[at, :], soft_ref[at, :]
        for i in range(COL_TILES):
            lanes = slice(LANES * i, LANES * (i + 1))
            grad_ref[at, lanes] = (exp_ref[at, lanes] * soft_rows - weighted_ref[at, lanes] * target_rows).astype(BF16)
        return carry

    lax.fori_loop(0, ROWS // 64, block, 0)

    for fetch in fetches:
        fetch.wait()
    half_block = (2, PAIRS, D // BATCH, CHUNK)
    for lo in range(0, COLS, CHUNK):
        lanes = slice(lo, lo + CHUNK)
        rows = order_ref[...].reshape(D, ROWS)
        part = jnp.dot(rows, grad_ref[:, lanes], preferred_element_type=F32)
        unit = raw_cols_ref[:, :, :, :, lanes].astype(F32).reshape(D, CHUNK) * cols_inv_ref[:, lanes]
        part = part - unit * jnp.sum(unit * part, axis=0, keepdims=True)
        own_ref[:, :, :, lanes] = part[: D // 2].reshape(half_block)
        other_ref[:, :, :, lanes] = part[D // 2 :].reshape(half_block)
    loss_row = jnp.full((2, PAIRS, D // BATCH, LANES), local_loss, F32)
    own_ref[:, :, :, COLS:] = loss_row
    other_ref[:, :, :, COLS:] = loss_row


def feat_grad_kernel(grad_ref, cols_ref, raw_feat_ref, feat_inv_ref, out_ref, stage_ref, sems):
    copies = []
    for quarter in range(4):
        lanes = slice(QUARTER * quarter, QUARTER * (quarter + 1))
        part = lax.dot_general(
            cols_ref[...], grad_ref[lanes, :], (((1,), (1,)), ((), ())), preferred_element_type=F32
        )
        unit = raw_feat_ref[:, lanes].astype(F32) * feat_inv_ref[:, lanes]
        part = part - unit * jnp.sum(unit * part, axis=0, keepdims=True)
        stage_ref[quarter] = part.reshape(PROTO, 8, QUARTER).astype(BF16)
        there = out_ref.at[:, :, pl.ds(QUARTER * quarter, QUARTER)]
        copies.append(pltpu.make_async_copy(stage_ref.at[quarter], there, sems.at[quarter]))
        copies[-1].start()
    for copy in copies:
        copy.wait()


def spread(tail):
    lane = lax.broadcasted_iota(jnp.int32, tail.shape, tail.ndim - 1)
    high = tail.astype(BF16).astype(F32)
    middle = (tail - high).astype(BF16).astype(F32)
    return jnp.where(lane == 0, high, jnp.where(lane == 1, middle, tail - high - middle)).astype(BF16)


def gather_parts(tail):
    return tail[..., 0:1] + tail[..., 1:2] + tail[..., 2:3]


def join_cores_kernel(own_ref, got_ref, feat_ref, keep_ref, send_ref, feat_out_ref):
    keep_ref[...] = own_ref[0] + got_ref[0]
    away = own_ref[1] + got_ref[1]
    send_ref[:, :, :COLS] = away[:, :, :COLS].astype(BF16)
    send_ref[:, :, COLS:] = spread(away[:, :, COLS:])


def join_pairs_kernel(place_ref, own_ref, got_ref, keep_ref, *send_refs):
    pair = lax.div(lax.div(place_ref[0], PROTO), 4)
    for away in range(PAIRS):
        there = lax.rem(pair + away, PAIRS)
        got = got_ref[there].astype(F32)
        total = own_ref[there, :, :COLS] + got[:, :COLS]
        tail = own_ref[there, :, COLS:] + gather_parts(got[:, COLS:])
        if away == 0:
            keep_ref[:, :COLS] = total
            keep_ref[:, COLS:] = tail
        else:
            send_refs[away - 1][:, :COLS] = total.astype(BF16)
            send_refs[away - 1][:, COLS:] = spread(tail)


def feat_sum_kernel(feat_ref, feat_out_ref):
    feat_out_ref[...] = jnp.sum(feat_ref[...].astype(F32), axis=0)


def proto_sum_kernel(keep_ref, first_ref, second_ref, third_ref, after_ref, proto_out_ref, loss_ref):
    total = keep_ref[:, :COLS]
    loss = keep_ref[0:1, COLS : COLS + 1]
    for ref in (first_ref, second_ref, third_ref):
        got = ref[...].astype(F32)
        total += got[:, :COLS]
        loss += gather_parts(got[0:1, COLS:])
    proto_out_ref[...] = total
    loss_ref[...] = loss / CROPS


def per_device(student_feat, teacher_feat, student_proto, teacher_proto):
    place = (lax.axis_index("batch") * PROTO + lax.axis_index("proto")).astype(jnp.int32).reshape(1)
    swap_cores = [(i, i ^ 1) for i in range(BATCH)]
    swap_pairs = [(i, i ^ 2) for i in range(BATCH)]
    swap_sides = [(i, i ^ SIDE) for i in range(PROTO)]

    def over_batch(array):
        return lax.all_to_all(array, "batch", 0, 0)

    def over_proto(array):
        return lax.all_to_all(array, "proto", 0, 0)

    packed = shape((PROTO, 8, ROWS), BF16)
    rounded = shape((D, COLS), BF16)
    row_shape = shape((PROTO, ROW_TILES, LANES), BF16)
    first_row_shape = shape((PROTO, ROW_TILES, HALF + LANES), BF16)
    last_shape = shape((PROTO, 5 * ROW_TILES, LANES), BF16)
    col_shape, last_col_shape = shape((BATCH, COL_TILES, LANES), BF16), shape((BATCH, COL_TILES, LANES))
    row_tile, row_part = pltpu.VMEM((ROW_TILES, LANES), F32), pltpu.VMEM((ROWS, LANES), F32)
    col_tile, col_part = pltpu.VMEM((COL_TILES, LANES), F32), pltpu.VMEM((8, COLS), F32)

    send, place = pl.pallas_call(
        prepare_kernel,
        out_shape=[packed, shape((1,), jnp.int32)],
        in_specs=[SM, VM],
        out_specs=[VM, SM],
        name="prepare",
    )(place, teacher_feat.T)
    teach = over_proto(send)
    teacher_cols, proto_round, proto_inv = call(
        unit_cols_kernel, [rounded, rounded, shape((1, COLS))], [teacher_proto, student_proto], name="unit_cols"
    )
    teacher_exp, send = call(
        teacher_kernel,
        [pinned((ROWS, COLS)), col_shape],
        [teach, teacher_cols],
        [pltpu.VMEM((ROWS, D), BF16), col_part],
        name="teacher_exp",
    )
    got = over_batch(send)
    (send,) = call(
        first_row_kernel,
        [first_row_shape],
        [pin(teacher_exp), got, student_feat.T],
        [col_tile, row_part, row_tile],
        name="row_pass_1",
    )
    own_half = over_proto(send)
    other_half = lax.ppermute(own_half, "proto", swap_sides)
    (send,) = call(
        col_kernel, [col_shape], [pin(teacher_exp), own_half], [row_part, col_part], name="col_pass_2"
    )
    got = over_batch(send)
    (send,) = call(
        row_kernel,
        [row_shape],
        [pin(teacher_exp), got, other_half],
        [col_tile, row_part, row_tile],
        specs=[VM, VM, ANY],
        name="row_pass_2",
    )
    got = over_proto(send)
    (send,) = call(col_kernel, [last_col_shape], [pin(teacher_exp), got], [row_part, col_part], name="col_pass_3")
    got = over_batch(send)
    student_exp, weighted, raw_feat, feat_round, feat_inv, send = call(
        student_kernel,
        [
            pinned((ROWS, COLS)),
            pinned((ROWS, COLS)),
            shape((D, ROWS), BF16),
            shape((D, ROWS), BF16),
            shape((1, ROWS)),
            last_shape,
        ],
        [place, own_half, other_half, pin(teacher_exp), proto_round, got],
        [pltpu.VMEM((ROWS, D), BF16), col_tile, row_part, row_part, row_part, row_tile],
        specs=[SM] + [VM] * 5,
        name="student_and_last_row",
    )
    got = over_proto(send)
    half_shape = shape((2, PAIRS, D // BATCH, COLS + LANES))
    split = (PAIRS, 2, 2, D // BATCH)
    order = (2, 2, PAIRS, D // BATCH)
    grad_logit, own, other = call(
        grad_kernel,
        [pinned((ROWS, COLS), BF16), half_shape, half_shape],
        [
            place,
            pin(weighted),
            pin(student_exp),
            feat_round.reshape(split + (ROWS,)),
            got,
            stay(student_proto.reshape(split + (COLS,))),
            proto_inv,
        ],
        [
            row_part,
            row_part,
            pltpu.VMEM(order + (ROWS,), BF16),
            pltpu.VMEM(order + (COLS,), BF16),
            pltpu.SemaphoreType.DMA((4,)),
        ],
        specs=[SM] + [VM] * 4 + [ANY, VM],
        vmem=16,
        name="proto_grad",
    )
    arrived = lax.ppermute(other, "batch", swap_cores)
    feat_part = pl.pallas_call(
        feat_grad_kernel,
        out_shape=packed,
        in_specs=[VM] * 4,
        out_specs=ANY,
        scratch_shapes=[pltpu.VMEM((4, PROTO, 8, QUARTER), BF16), pltpu.SemaphoreType.DMA((4,))],
        compiler_params=pltpu.CompilerParams(vmem_limit_bytes=12 * MIB),
        name="feat_grad",
    )(pin(grad_logit), proto_round, raw_feat, feat_inv)
    pair_shape = (PAIRS, D // BATCH, COLS + LANES)
    keep, send, feat_part = pl.pallas_call(
        join_cores_kernel,
        out_shape=[shape(pair_shape), shape(pair_shape, BF16), packed],
        in_specs=[VM, VM, ANY],
        out_specs=[VM, VM, ANY],
        input_output_aliases={2: 2},
        compiler_params=pltpu.CompilerParams(vmem_limit_bytes=12 * MIB),
        name="join_cores",
    )(own, arrived, feat_part)
    feat_got = over_proto(feat_part)
    arrived = lax.ppermute(send, "batch", swap_pairs)
    block = pair_shape[1:]
    keep, *sends = call(
        join_pairs_kernel,
        [shape(block)] + [shape(block, BF16)] * (PAIRS - 1),
        [place, keep, arrived],
        specs=[SM, VM, VM],
        flops=LONG,
        name="join_pairs",
    )
    quads = [
        lax.ppermute(send, "batch", [(i, (i + 4 * away) % BATCH) for i in range(BATCH)])
        for away, send in enumerate(sends, 1)
    ]
    (feat_out,) = call(feat_sum_kernel, [shape((8, ROWS))], [feat_got], name="feat_sum")
    proto_out, loss = call(
        proto_sum_kernel,
        [shape((D // BATCH, COLS)), shape((1, 1))],
        [keep, *quads, feat_out],
        specs=[VM] * 4 + [ANY],
        name="proto_sum",
    )
    return (loss.reshape(()), feat_out.T, proto_out)


def solution(mesh):
    placed = (P("batch", "proto"), P("batch", "proto"), P(None, "proto"), P(None, "proto"))
    return jax.shard_map(
        per_device,
        mesh=mesh,
        in_specs=placed,
        out_specs=(P(), P("batch", "proto"), P("batch", "proto")),
        check_vma=False,
    )
```

```python
import jax
import jax.numpy as jnp
from jax import lax
from jax.experimental import pallas as pl
from jax.experimental.pallas import tpu as pltpu
from jax.sharding import PartitionSpec as P

F32, BF16 = jnp.float32, jnp.bfloat16
SWEEPS = 3
LOG2E = 1.4426950408889634
STUDENT_SCALE = LOG2E / 0.1
TEACHER_SCALE = LOG2E / 0.07
D, ROWS, COLS = 256, 1024, 2048
LANES = 128
ROW_TILES, COL_TILES = ROWS // LANES, COLS // LANES
PROTO, BATCH = 32, 16
PAIRS = BATCH // 4
SIDE = 8
CROPS, PROTOS = ROWS * BATCH, COLS * PROTO
HALF = ROWS // 2
QUARTER = ROWS // 4
CHUNK = 512
BAND = 32
MIB = 1024 * 1024
LONG = 200_000_000_000

VM = pl.BlockSpec(memory_space=pltpu.VMEM)
ANY = pl.BlockSpec(memory_space=pl.ANY)


def shape(dims, dtype=F32):
    return jax.ShapeDtypeStruct(dims, dtype)


def pinned(dims, dtype=F32):
    return pltpu.VMEM(dims, dtype)


def pin(array):
    return pltpu.with_memory_space_constraint(array, pltpu.VMEM)


def stay(array):
    return pltpu.with_memory_space_constraint(array, pltpu.HBM)


def call(body, outs, args, scratch=(), specs=None, name=None, vmem=12, aliases=None, flops=None):
    return pl.pallas_call(
        body,
        out_shape=outs,
        in_specs=specs or [VM] * len(args),
        out_specs=[VM] * len(outs),
        scratch_shapes=list(scratch),
        compiler_params=pltpu.CompilerParams(vmem_limit_bytes=vmem * MIB),
        input_output_aliases=aliases or {},
        cost_estimate=flops and pl.CostEstimate(flops=flops, bytes_accessed=0, transcendentals=0),
        name=name,
    )(*args)


def lane_major(partial_ref, out_ref):
    for j in range(ROW_TILES):
        tile = partial_ref[LANES * j : LANES * (j + 1), :]
        out_ref[j : j + 1, :] = jnp.sum(tile.T, axis=0, keepdims=True)


def sublane_major(values, out_ref):
    for j in range(ROW_TILES):
        out_ref[LANES * j : LANES * (j + 1), :] = jnp.broadcast_to(values[j : j + 1, :], (LANES, LANES)).T


def prepare_kernel(teach_ref, teach_out):
    put(teach_out, teach_ref[...])


def unit_cols_kernel(teacher_ref, student_ref, teacher_out, student_out, inv_ref):
    for lo in range(0, COLS, CHUNK):
        lanes = slice(lo, lo + CHUNK)
        teacher_out[:, lanes] = unit_rows(teacher_ref[:, lanes].astype(F32)).astype(BF16)
        x = student_ref[:, lanes].astype(F32)
        inv = lax.rsqrt(jnp.sum(x * x, axis=0, keepdims=True) + 1e-06)
        inv_ref[:, lanes] = inv
        student_out[:, lanes] = (x * inv).astype(BF16)


def unit_rows(x):
    return x * lax.rsqrt(jnp.sum(x * x, axis=0, keepdims=True) + 1e-06)


def put(out_ref, value, rows=slice(None), lanes=slice(None)):
    for peer in range(out_ref.shape[0]):
        out_ref[peer, rows, lanes] = value


def col_rows(acc_ref):
    total = jnp.sum(acc_ref[...], axis=0, keepdims=True)
    return jnp.concatenate([total[:, LANES * i : LANES * (i + 1)] for i in range(COL_TILES)], axis=0)


def row_block(j):
    return pl.ds(pl.multiple_of(j * LANES, LANES), LANES)


def teacher_kernel(feat_ref, cols_ref, exp_ref, out_ref, rows_ref, acc_ref):
    for half in range(2):
        lanes = slice(HALF * half, HALF * (half + 1))
        x = feat_ref[:, :, lanes].astype(F32).reshape(D, HALF)
        rows_ref[lanes, :] = unit_rows(x).T.astype(BF16)
    for lo in range(0, COLS, CHUNK):
        lanes = slice(lo, lo + CHUNK)
        z = jnp.dot(rows_ref[...], cols_ref[:, lanes], preferred_element_type=F32)
        e = jnp.exp2(z * TEACHER_SCALE)
        exp_ref[:, lanes] = e
        acc_ref[:, lanes] = jnp.sum(e.reshape(ROWS // 8, 8, CHUNK), axis=0)
    put(out_ref, col_rows(acc_ref).astype(out_ref.dtype))


def col_scale_of(got_ref):
    return 1.0 / (PROTOS * jnp.sum(got_ref[...].astype(F32), axis=0))


def row_sums(exp_ref, scale_ref, part_ref, sum_ref):
    def block(pair, carry):
        for j in (2 * pair, 2 * pair + 1):
            at = row_block(j)
            acc = jnp.zeros((LANES, LANES), F32)
            for i in range(COL_TILES):
                acc += exp_ref[at, LANES * i : LANES * (i + 1)] * scale_ref[i : i + 1, :]
            part_ref[at, :] = acc
        return carry

    lax.fori_loop(0, ROW_TILES // 2, block, 0)
    lane_major(part_ref, sum_ref)


def first_row_kernel(exp_ref, got_ref, stud_ref, out_ref, scale_ref, part_ref, sum_ref):
    scale_ref[...] = col_scale_of(got_ref)
    row_sums(exp_ref, scale_ref, part_ref, sum_ref)
    sums = sum_ref[...].astype(BF16)
    for peer in range(PROTO):
        half = peer // SIDE % 2
        out_ref[peer, :, :HALF] = stud_ref[:, HALF * half : HALF * (half + 1)]
        out_ref[peer, :, HALF:] = sums


def row_kernel(exp_ref, got_ref, after_ref, out_ref, scale_ref, part_ref, sum_ref):
    scale_ref[...] = col_scale_of(got_ref)
    row_sums(exp_ref, scale_ref, part_ref, sum_ref)
    put(out_ref, sum_ref[...].astype(BF16))


def col_kernel(exp_ref, got_ref, out_ref, rows_ref, acc_ref):
    sublane_major(1.0 / (CROPS * jnp.sum(got_ref[:, :, -LANES:].astype(F32), axis=0)), rows_ref)
    acc_ref[...] = jnp.zeros_like(acc_ref)

    def block(j, carry):
        at = row_block(j)
        r = rows_ref[at, :]
        for i in range(COL_TILES):
            lanes = slice(LANES * i, LANES * (i + 1))
            acc_ref[:, lanes] += jnp.sum((exp_ref[at, lanes] * r).reshape(LANES // 8, 8, LANES), axis=0)
        return carry

    lax.fori_loop(0, ROW_TILES, block, 0)
    put(out_ref, col_rows(acc_ref).astype(out_ref.dtype))


def student_kernel(
    own_ref, other_ref, teacher_ref, cols_ref, got_ref, exp_ref, weighted_ref, raw_feat_ref, feat_out_ref, feat_inv_ref,
    out_ref, rows_ref, scale_ref, part_ref, cross_ref, total_ref, sum_ref,
):
    scale_ref[...] = col_scale_of(got_ref)
    side = lax.rem(lax.div(lax.axis_index("proto"), SIDE), 2)
    for half in range(2):
        lanes = slice(HALF * half, HALF * (half + 1))
        own, other = own_ref[:, :, :HALF].astype(F32), other_ref[:, :, :HALF].astype(F32)
        x = jnp.where(side == half, own, other).reshape(D, HALF)
        raw_feat_ref[:, lanes] = x.astype(BF16)
        inv = lax.rsqrt(jnp.sum(x * x, axis=0, keepdims=True) + 1e-06)
        unit = x * inv
        rows_ref[lanes, :] = unit.T.astype(BF16)
        feat_out_ref[:, lanes] = unit.astype(BF16)
        feat_inv_ref[:, lanes] = inv

    for lo in range(0, COLS, CHUNK):
        z = jnp.dot(rows_ref[...], cols_ref[:, lo : lo + CHUNK], preferred_element_type=F32)
        for top in range(0, ROWS, BAND):
            band = slice(top, top + BAND)
            if lo == 0:
                acc = cross = total = jnp.zeros((BAND, LANES), F32)
            else:
                acc, cross, total = part_ref[band, :], cross_ref[band, :], total_ref[band, :]
            for i in range(lo // LANES, (lo + CHUNK) // LANES):
                lanes = slice(LANES * i, LANES * (i + 1))
                logit = z[band, LANES * i - lo : LANES * (i + 1) - lo]
                e = jnp.exp2(logit * STUDENT_SCALE)
                exp_ref[band, lanes] = e
                weighted = teacher_ref[band, lanes] * scale_ref[i : i + 1, :]
                weighted_ref[band, lanes] = weighted
                acc += weighted
                cross += weighted * logit
                total += e
            part_ref[band, :], cross_ref[band, :], total_ref[band, :] = acc, cross, total
    sends = []
    for ref in (part_ref, total_ref, cross_ref):
        lane_major(ref, sum_ref)
        high = sum_ref[...].astype(BF16).astype(F32)
        sends += [high, sum_ref[...] - high]
    put(out_ref, jnp.concatenate(sends[:5], axis=0).astype(BF16))


def grad_kernel(
    weighted_ref, exp_ref, feat_ref, got_ref, source_ref, cols_inv_ref,
    grad_ref, own_ref, other_ref, target_ref, soft_ref, order_ref, raw_cols_ref, sems,
):
    batch = lax.axis_index("batch")
    core, odd = lax.rem(batch, 2), lax.rem(lax.div(batch, 2), 2)
    fetches = []
    for away in range(2):
        parity = odd if away == 0 else 1 - odd
        for side in range(2):
            other = core if side == 0 else 1 - core
            fetches.append(
                pltpu.make_async_copy(source_ref.at[:, parity, other], raw_cols_ref.at[side, away], sems.at[len(fetches)])
            )
            for pair in range(PAIRS):
                order_ref[side, away, pair] = feat_ref[pair, parity, other]
    for fetch in fetches:
        fetch.start()
    got = jnp.sum(got_ref[...].astype(F32), axis=0).reshape(5, ROW_TILES, LANES)
    sums, totals, cross = got[0] + got[1], got[2] + got[3], got[4] / 0.1
    local_loss = jnp.sum(jnp.log(totals) - cross / sums)
    sublane_major(PROTOS / sums, target_ref)
    sublane_major(PROTOS / totals, soft_ref)

    def block(j, carry):
        at = pl.ds(pl.multiple_of(j * 64, 64), 64)
        target_rows, soft_rows = target_ref[at, :], soft_ref[at, :]
        for i in range(COL_TILES):
            lanes = slice(LANES * i, LANES * (i + 1))
            grad_ref[at, lanes] = (exp_ref[at, lanes] * soft_rows - weighted_ref[at, lanes] * target_rows).astype(BF16)
        return carry

    lax.fori_loop(0, ROWS // 64, block, 0)

    for fetch in fetches:
        fetch.wait()
    half_block = (2, PAIRS, D // BATCH, CHUNK)
    for lo in range(0, COLS, CHUNK):
        lanes = slice(lo, lo + CHUNK)
        rows = order_ref[...].reshape(D, ROWS)
        part = jnp.dot(rows, grad_ref[:, lanes], preferred_element_type=F32)
        unit = raw_cols_ref[:, :, :, :, lanes].astype(F32).reshape(D, CHUNK) * cols_inv_ref[:, lanes]
        part = part - unit * jnp.sum(unit * part, axis=0, keepdims=True)
        own_ref[:, :, :, lanes] = part[: D // 2].reshape(half_block)
        other_ref[:, :, :, lanes] = part[D // 2 :].reshape(half_block)
    loss_row = jnp.full((2, PAIRS, D // BATCH, LANES), local_loss, F32)
    own_ref[:, :, :, COLS:] = loss_row
    other_ref[:, :, :, COLS:] = loss_row


def feat_grad_kernel(grad_ref, cols_ref, raw_feat_ref, feat_inv_ref, out_ref, stage_ref, sems):
    copies = []
    for side in range(2):
        parts = []
        for half in range(2):
            lanes = slice(HALF * half + QUARTER * side, HALF * half + QUARTER * (side + 1))
            part = lax.dot_general(
                cols_ref[...], grad_ref[lanes, :], (((1,), (1,)), ((), ())), preferred_element_type=F32
            )
            unit = raw_feat_ref[:, lanes].astype(F32) * feat_inv_ref[:, lanes]
            part = part - unit * jnp.sum(unit * part, axis=0, keepdims=True)
            parts.append(part.reshape(PROTO, 8, QUARTER))
        stage_ref[side] = jnp.concatenate(parts, axis=1).astype(BF16)
        there = out_ref.at[:, :, pl.ds(QUARTER * side, QUARTER)]
        copies.append(pltpu.make_async_copy(stage_ref.at[side], there, sems.at[side]))
        copies[-1].start()
    for copy in copies:
        copy.wait()


def spread(tail):
    lane = lax.broadcasted_iota(jnp.int32, tail.shape, tail.ndim - 1)
    high = tail.astype(BF16).astype(F32)
    middle = (tail - high).astype(BF16).astype(F32)
    return jnp.where(lane == 0, high, jnp.where(lane == 1, middle, tail - high - middle)).astype(BF16)


def gather_parts(tail):
    return tail[..., 0:1] + tail[..., 1:2] + tail[..., 2:3]


def join_cores_kernel(own_ref, got_ref, feat_ref, keep_ref, send_ref, feat_out_ref):
    keep_ref[...] = own_ref[0] + got_ref[0]
    away = own_ref[1] + got_ref[1]
    send_ref[:, :, :COLS] = away[:, :, :COLS].astype(BF16)
    send_ref[:, :, COLS:] = spread(away[:, :, COLS:])


def join_pairs_kernel(own_ref, got_ref, keep_ref, *send_refs):
    pair = lax.div(lax.axis_index("batch"), 4)
    for away in range(PAIRS):
        there = lax.rem(pair + away, PAIRS)
        got = got_ref[there].astype(F32)
        total = own_ref[there, :, :COLS] + got[:, :COLS]
        tail = own_ref[there, :, COLS:] + gather_parts(got[:, COLS:])
        if away == 0:
            keep_ref[:, :COLS] = total
            keep_ref[:, COLS:] = tail
        else:
            send_refs[away - 1][:, :COLS] = total.astype(BF16)
            send_refs[away - 1][:, COLS:] = spread(tail)


def feat_sum_kernel(feat_ref, feat_out_ref):
    total = jnp.sum(feat_ref[...].astype(F32), axis=0)
    feat_out_ref[:, :HALF] = total[:8]
    feat_out_ref[:, HALF:] = total[8:]


def proto_sum_kernel(keep_ref, first_ref, second_ref, third_ref, after_ref, proto_out_ref, loss_ref):
    total = keep_ref[:, :COLS]
    loss = keep_ref[0:1, COLS : COLS + 1]
    for ref in (first_ref, second_ref, third_ref):
        got = ref[...].astype(F32)
        total += got[:, :COLS]
        loss += gather_parts(got[0:1, COLS:])
    proto_out_ref[...] = total
    loss_ref[...] = loss / CROPS


def per_device(student_feat, teacher_feat, student_proto, teacher_proto):
    swap_cores = [(i, i ^ 1) for i in range(BATCH)]
    swap_pairs = [(i, i ^ 2) for i in range(BATCH)]
    swap_sides = [(i, i ^ SIDE) for i in range(PROTO)]

    def over_batch(array):
        return lax.all_to_all(array, "batch", 0, 0)

    def over_proto(array):
        return lax.all_to_all(array, "proto", 0, 0)

    packed, halved = shape((PROTO, 8, ROWS), BF16), shape((PROTO, 16, HALF), BF16)
    rounded = shape((D, COLS), BF16)
    row_shape = shape((PROTO, ROW_TILES, LANES), BF16)
    first_row_shape = shape((PROTO, ROW_TILES, HALF + LANES), BF16)
    last_shape = shape((PROTO, 5 * ROW_TILES, LANES), BF16)
    col_shape, last_col_shape = shape((BATCH, COL_TILES, LANES), BF16), shape((BATCH, COL_TILES, LANES))
    row_tile, row_part = pltpu.VMEM((ROW_TILES, LANES), F32), pltpu.VMEM((ROWS, LANES), F32)
    col_tile, col_part = pltpu.VMEM((COL_TILES, LANES), F32), pltpu.VMEM((8, COLS), F32)

    (send,) = call(prepare_kernel, [packed], [teacher_feat.T], name="prepare")
    teach = over_proto(send)
    teacher_cols, proto_round, proto_inv = call(
        unit_cols_kernel, [rounded, rounded, shape((1, COLS))], [teacher_proto, student_proto], name="unit_cols"
    )
    teacher_exp, send = call(
        teacher_kernel,
        [pinned((ROWS, COLS)), col_shape],
        [teach, teacher_cols],
        [pltpu.VMEM((ROWS, D), BF16), col_part],
        name="teacher_exp",
    )
    got = over_batch(send)
    (send,) = call(
        first_row_kernel,
        [first_row_shape],
        [pin(teacher_exp), got, student_feat.T],
        [col_tile, row_part, row_tile],
        name="row_pass_1",
    )
    own_half = over_proto(send)
    other_half = lax.ppermute(own_half, "proto", swap_sides)
    (send,) = call(
        col_kernel, [col_shape], [pin(teacher_exp), own_half], [row_part, col_part], name="col_pass_2"
    )
    got = over_batch(send)
    (send,) = call(
        row_kernel,
        [row_shape],
        [pin(teacher_exp), got, other_half],
        [col_tile, row_part, row_tile],
        specs=[VM, VM, ANY],
        name="row_pass_2",
    )
    got = over_proto(send)
    (send,) = call(col_kernel, [last_col_shape], [pin(teacher_exp), got], [row_part, col_part], name="col_pass_3")
    got = over_batch(send)
    student_exp, weighted, raw_feat, feat_round, feat_inv, send = call(
        student_kernel,
        [
            pinned((ROWS, COLS)),
            pinned((ROWS, COLS)),
            shape((D, ROWS), BF16),
            shape((D, ROWS), BF16),
            shape((1, ROWS)),
            last_shape,
        ],
        [own_half, other_half, pin(teacher_exp), proto_round, got],
        [pltpu.VMEM((ROWS, D), BF16), col_tile, row_part, row_part, row_part, row_tile],
        name="student_and_last_row",
    )
    got = over_proto(send)
    half_shape = shape((2, PAIRS, D // BATCH, COLS + LANES))
    split = (PAIRS, 2, 2, D // BATCH)
    order = (2, 2, PAIRS, D // BATCH)
    grad_logit, own, other = call(
        grad_kernel,
        [pinned((ROWS, COLS), BF16), half_shape, half_shape],
        [
            pin(weighted),
            pin(student_exp),
            feat_round.reshape(split + (ROWS,)),
            got,
            stay(student_proto.reshape(split + (COLS,))),
            proto_inv,
        ],
        [
            row_part,
            row_part,
            pltpu.VMEM(order + (ROWS,), BF16),
            pltpu.VMEM(order + (COLS,), BF16),
            pltpu.SemaphoreType.DMA((4,)),
        ],
        specs=[VM] * 4 + [ANY, VM],
        vmem=16,
        name="proto_grad",
    )
    arrived = lax.ppermute(other, "batch", swap_cores)
    feat_part = pl.pallas_call(
        feat_grad_kernel,
        out_shape=halved,
        in_specs=[VM] * 4,
        out_specs=ANY,
        scratch_shapes=[pltpu.VMEM((2, PROTO, 16, QUARTER), BF16), pltpu.SemaphoreType.DMA((2,))],
        compiler_params=pltpu.CompilerParams(vmem_limit_bytes=12 * MIB),
        name="feat_grad",
    )(pin(grad_logit), proto_round, raw_feat, feat_inv)
    pair_shape = (PAIRS, D // BATCH, COLS + LANES)
    keep, send, feat_part = pl.pallas_call(
        join_cores_kernel,
        out_shape=[shape(pair_shape), shape(pair_shape, BF16), halved],
        in_specs=[VM, VM, ANY],
        out_specs=[VM, VM, ANY],
        input_output_aliases={2: 2},
        compiler_params=pltpu.CompilerParams(vmem_limit_bytes=12 * MIB),
        name="join_cores",
    )(own, arrived, feat_part)
    feat_got = over_proto(feat_part)
    arrived = lax.ppermute(send, "batch", swap_pairs)
    block = pair_shape[1:]
    keep, *sends = call(
        join_pairs_kernel,
        [shape(block)] + [shape(block, BF16)] * (PAIRS - 1),
        [keep, arrived],
        flops=LONG,
        name="join_pairs",
    )
    quads = [
        lax.ppermute(send, "batch", [(i, (i + 4 * away) % BATCH) for i in range(BATCH)])
        for away, send in enumerate(sends, 1)
    ]
    (feat_out,) = call(feat_sum_kernel, [shape((8, ROWS))], [feat_got], name="feat_sum")
    proto_out, loss = call(
        proto_sum_kernel,
        [shape((D // BATCH, COLS)), shape((1, 1))],
        [keep, *quads, feat_out],
        specs=[VM] * 4 + [ANY],
        name="proto_sum",
    )
    return (loss.reshape(()), feat_out.T, proto_out)


def solution(mesh):
    placed = (P("batch", "proto"), P("batch", "proto"), P(None, "proto"), P(None, "proto"))
    return jax.shard_map(
        per_device,
        mesh=mesh,
        in_specs=placed,
        out_specs=(P(), P("batch", "proto"), P("batch", "proto")),
        check_vma=False,
    )
```

```python
import jax
import jax.numpy as jnp
from jax import lax
from jax.experimental import pallas as pl
from jax.experimental.pallas import tpu as pltpu
from jax.sharding import PartitionSpec as P

F32, BF16 = jnp.float32, jnp.bfloat16
SWEEPS = 3
LOG2E = 1.4426950408889634
STUDENT_SCALE = LOG2E / 0.1
TEACHER_SCALE = LOG2E / 0.07
D, ROWS, COLS = 256, 1024, 2048
LANES = 128
ROW_TILES, COL_TILES = ROWS // LANES, COLS // LANES
PROTO, BATCH = 32, 16
PAIRS = BATCH // 4
SIDE = 8
CROPS, PROTOS = ROWS * BATCH, COLS * PROTO
HALF = ROWS // 2
QUARTER = ROWS // 4
CHUNK = 512
BAND = 32
MIB = 1024 * 1024
LONG = 200_000_000_000

VM = pl.BlockSpec(memory_space=pltpu.VMEM)
ANY = pl.BlockSpec(memory_space=pl.ANY)


def shape(dims, dtype=F32):
    return jax.ShapeDtypeStruct(dims, dtype)


def pinned(dims, dtype=F32):
    return pltpu.VMEM(dims, dtype)


def pin(array):
    return pltpu.with_memory_space_constraint(array, pltpu.VMEM)


def stay(array):
    return pltpu.with_memory_space_constraint(array, pltpu.HBM)


def call(body, outs, args, scratch=(), specs=None, name=None, vmem=12, aliases=None, flops=None):
    return pl.pallas_call(
        body,
        out_shape=outs,
        in_specs=specs or [VM] * len(args),
        out_specs=[VM] * len(outs),
        scratch_shapes=list(scratch),
        compiler_params=pltpu.CompilerParams(vmem_limit_bytes=vmem * MIB),
        input_output_aliases=aliases or {},
        cost_estimate=flops and pl.CostEstimate(flops=flops, bytes_accessed=0, transcendentals=0),
        name=name,
    )(*args)


def lane_major(partial_ref, out_ref):
    for j in range(ROW_TILES):
        tile = partial_ref[LANES * j : LANES * (j + 1), :]
        out_ref[j : j + 1, :] = jnp.sum(tile.T, axis=0, keepdims=True)


def sublane_major(values, out_ref):
    for j in range(ROW_TILES):
        out_ref[LANES * j : LANES * (j + 1), :] = jnp.broadcast_to(values[j : j + 1, :], (LANES, LANES)).T


def prepare_kernel(teach_ref, teach_out):
    put(teach_out, teach_ref[...])


def unit_cols_kernel(teacher_ref, student_ref, teacher_out, student_out, inv_ref):
    for lo in range(0, COLS, CHUNK):
        lanes = slice(lo, lo + CHUNK)
        teacher_out[:, lanes] = unit_rows(teacher_ref[:, lanes].astype(F32)).astype(BF16)
        x = student_ref[:, lanes].astype(F32)
        inv = lax.rsqrt(jnp.sum(x * x, axis=0, keepdims=True) + 1e-06)
        inv_ref[:, lanes] = inv
        student_out[:, lanes] = (x * inv).astype(BF16)


def unit_rows(x):
    return x * lax.rsqrt(jnp.sum(x * x, axis=0, keepdims=True) + 1e-06)


def put(out_ref, value, rows=slice(None), lanes=slice(None)):
    for peer in range(out_ref.shape[0]):
        out_ref[peer, rows, lanes] = value


def col_rows(acc_ref):
    total = jnp.sum(acc_ref[...], axis=0, keepdims=True)
    return jnp.concatenate([total[:, LANES * i : LANES * (i + 1)] for i in range(COL_TILES)], axis=0)


def row_block(j):
    return pl.ds(pl.multiple_of(j * LANES, LANES), LANES)


def teacher_kernel(feat_ref, cols_ref, exp_ref, out_ref, rows_ref, acc_ref):
    for half in range(2):
        lanes = slice(HALF * half, HALF * (half + 1))
        x = feat_ref[:, :, lanes].astype(F32).reshape(D, HALF)
        rows_ref[lanes, :] = unit_rows(x).T.astype(BF16)
    for lo in range(0, COLS, CHUNK):
        lanes = slice(lo, lo + CHUNK)
        z = jnp.dot(rows_ref[...], cols_ref[:, lanes], preferred_element_type=F32)
        e = jnp.exp2(z * TEACHER_SCALE)
        exp_ref[:, lanes] = e
        acc_ref[:, lanes] = jnp.sum(e.reshape(ROWS // 8, 8, CHUNK), axis=0)
    put(out_ref, col_rows(acc_ref).astype(out_ref.dtype))


def col_scale_of(got_ref):
    return 1.0 / (PROTOS * jnp.sum(got_ref[...].astype(F32), axis=0))


def row_sums(exp_ref, scale_ref, part_ref, sum_ref):
    def block(pair, carry):
        for j in (2 * pair, 2 * pair + 1):
            at = row_block(j)
            acc = jnp.zeros((LANES, LANES), F32)
            for i in range(COL_TILES):
                acc += exp_ref[at, LANES * i : LANES * (i + 1)] * scale_ref[i : i + 1, :]
            part_ref[at, :] = acc
        return carry

    lax.fori_loop(0, ROW_TILES // 2, block, 0)
    lane_major(part_ref, sum_ref)


def first_row_kernel(exp_ref, got_ref, stud_ref, out_ref, scale_ref, part_ref, sum_ref):
    scale_ref[...] = col_scale_of(got_ref)
    row_sums(exp_ref, scale_ref, part_ref, sum_ref)
    sums = sum_ref[...].astype(BF16)
    for peer in range(PROTO):
        half = peer // SIDE % 2
        out_ref[peer, :, :HALF] = stud_ref[:, HALF * half : HALF * (half + 1)]
        out_ref[peer, :, HALF:] = sums


def row_kernel(exp_ref, got_ref, after_ref, out_ref, scale_ref, part_ref, sum_ref):
    scale_ref[...] = col_scale_of(got_ref)
    row_sums(exp_ref, scale_ref, part_ref, sum_ref)
    put(out_ref, sum_ref[...].astype(BF16))


def col_kernel(exp_ref, got_ref, out_ref, rows_ref, acc_ref):
    sublane_major(1.0 / (CROPS * jnp.sum(got_ref[:, :, -LANES:].astype(F32), axis=0)), rows_ref)
    acc_ref[...] = jnp.zeros_like(acc_ref)

    def block(j, carry):
        at = row_block(j)
        r = rows_ref[at, :]
        for i in range(COL_TILES):
            lanes = slice(LANES * i, LANES * (i + 1))
            acc_ref[:, lanes] += jnp.sum((exp_ref[at, lanes] * r).reshape(LANES // 8, 8, LANES), axis=0)
        return carry

    lax.fori_loop(0, ROW_TILES, block, 0)
    put(out_ref, col_rows(acc_ref).astype(out_ref.dtype))


def student_kernel(
    own_ref, other_ref, teacher_ref, cols_ref, got_ref, exp_ref, weighted_ref, raw_feat_ref, feat_out_ref, feat_inv_ref,
    out_ref, rows_ref, scale_ref, part_ref, cross_ref, total_ref, sum_ref,
):
    scale_ref[...] = col_scale_of(got_ref)
    side = lax.rem(lax.div(lax.axis_index("proto"), SIDE), 2)
    for half in range(2):
        lanes = slice(HALF * half, HALF * (half + 1))
        own, other = own_ref[:, :, :HALF].astype(F32), other_ref[:, :, :HALF].astype(F32)
        x = jnp.where(side == half, own, other).reshape(D, HALF)
        raw_feat_ref[:, lanes] = x.astype(BF16)
        inv = lax.rsqrt(jnp.sum(x * x, axis=0, keepdims=True) + 1e-06)
        unit = x * inv
        rows_ref[lanes, :] = unit.T.astype(BF16)
        feat_out_ref[:, lanes] = unit.astype(BF16)
        feat_inv_ref[:, lanes] = inv

    for lo in range(0, COLS, CHUNK):
        z = jnp.dot(rows_ref[...], cols_ref[:, lo : lo + CHUNK], preferred_element_type=F32)
        for top in range(0, ROWS, BAND):
            band = slice(top, top + BAND)
            if lo == 0:
                acc = cross = total = jnp.zeros((BAND, LANES), F32)
            else:
                acc, cross, total = part_ref[band, :], cross_ref[band, :], total_ref[band, :]
            for i in range(lo // LANES, (lo + CHUNK) // LANES):
                lanes = slice(LANES * i, LANES * (i + 1))
                logit = z[band, LANES * i - lo : LANES * (i + 1) - lo]
                e = jnp.exp2(logit * STUDENT_SCALE)
                exp_ref[band, lanes] = e
                weighted = teacher_ref[band, lanes] * scale_ref[i : i + 1, :]
                weighted_ref[band, lanes] = weighted
                acc += weighted
                cross += weighted * logit
                total += e
            part_ref[band, :], cross_ref[band, :], total_ref[band, :] = acc, cross, total
    sends = []
    for ref in (part_ref, total_ref, cross_ref):
        lane_major(ref, sum_ref)
        high = sum_ref[...].astype(BF16).astype(F32)
        sends += [high, sum_ref[...] - high]
    put(out_ref, jnp.concatenate(sends[:5], axis=0).astype(BF16))


def grad_kernel(
    weighted_ref, exp_ref, feat_ref, got_ref, source_ref, cols_inv_ref,
    grad_ref, own_ref, other_ref, target_ref, soft_ref, order_ref, raw_cols_ref, sems,
):
    batch = lax.axis_index("batch")
    core, odd = lax.rem(batch, 2), lax.rem(lax.div(batch, 2), 2)
    fetches = []
    for away in range(2):
        parity = odd if away == 0 else 1 - odd
        for side in range(2):
            other = core if side == 0 else 1 - core
            fetches.append(
                pltpu.make_async_copy(source_ref.at[:, parity, other], raw_cols_ref.at[side, away], sems.at[len(fetches)])
            )
            for pair in range(PAIRS):
                order_ref[side, away, pair] = feat_ref[pair, parity, other]
    for fetch in fetches:
        fetch.start()
    got = jnp.sum(got_ref[...].astype(F32), axis=0).reshape(5, ROW_TILES, LANES)
    sums, totals, cross = got[0] + got[1], got[2] + got[3], got[4] / 0.1
    local_loss = jnp.sum(jnp.log(totals) - cross / sums)
    sublane_major(PROTOS / sums, target_ref)
    sublane_major(PROTOS / totals, soft_ref)

    def block(j, carry):
        at = pl.ds(pl.multiple_of(j * 64, 64), 64)
        target_rows, soft_rows = target_ref[at, :], soft_ref[at, :]
        for i in range(COL_TILES):
            lanes = slice(LANES * i, LANES * (i + 1))
            grad_ref[at, lanes] = (exp_ref[at, lanes] * soft_rows - weighted_ref[at, lanes] * target_rows).astype(BF16)
        return carry

    lax.fori_loop(0, ROWS // 64, block, 0)

    for fetch in fetches:
        fetch.wait()
    half_block = (2, PAIRS, D // BATCH, CHUNK)
    for lo in range(0, COLS, CHUNK):
        lanes = slice(lo, lo + CHUNK)
        rows = order_ref[...].reshape(D, ROWS)
        part = jnp.dot(rows, grad_ref[:, lanes], preferred_element_type=F32)
        unit = raw_cols_ref[:, :, :, :, lanes].astype(F32).reshape(D, CHUNK) * cols_inv_ref[:, lanes]
        part = part - unit * jnp.sum(unit * part, axis=0, keepdims=True)
        own_ref[:, :, :, lanes] = part[: D // 2].reshape(half_block)
        other_ref[:, :, :, lanes] = part[D // 2 :].reshape(half_block)
    loss_row = jnp.full((2, PAIRS, D // BATCH, LANES), local_loss, F32)
    own_ref[:, :, :, COLS:] = loss_row
    other_ref[:, :, :, COLS:] = loss_row


def feat_grad_kernel(grad_ref, cols_ref, raw_feat_ref, feat_inv_ref, out_ref, stage_ref, sems):
    copies = []
    for side in range(2):
        parts = []
        for half in range(2):
            lanes = slice(HALF * half + QUARTER * side, HALF * half + QUARTER * (side + 1))
            part = lax.dot_general(
                cols_ref[...], grad_ref[lanes, :], (((1,), (1,)), ((), ())), preferred_element_type=F32
            )
            unit = raw_feat_ref[:, lanes].astype(F32) * feat_inv_ref[:, lanes]
            part = part - unit * jnp.sum(unit * part, axis=0, keepdims=True)
            parts.append(part.reshape(PROTO, 8, QUARTER))
        stage_ref[side] = jnp.concatenate(parts, axis=1).astype(BF16)
        there = out_ref.at[:, :, pl.ds(QUARTER * side, QUARTER)]
        copies.append(pltpu.make_async_copy(stage_ref.at[side], there, sems.at[side]))
        copies[-1].start()
    for copy in copies:
        copy.wait()


def spread(tail):
    lane = lax.broadcasted_iota(jnp.int32, tail.shape, tail.ndim - 1)
    high = tail.astype(BF16).astype(F32)
    middle = (tail - high).astype(BF16).astype(F32)
    return jnp.where(lane == 0, high, jnp.where(lane == 1, middle, tail - high - middle)).astype(BF16)


def gather_parts(tail):
    return tail[..., 0:1] + tail[..., 1:2] + tail[..., 2:3]


def join_cores_kernel(own_ref, got_ref, feat_ref, keep_ref, send_ref, feat_out_ref):
    keep_ref[...] = own_ref[0] + got_ref[0]
    away = own_ref[1] + got_ref[1]
    send_ref[:, :, :COLS] = away[:, :, :COLS].astype(BF16)
    send_ref[:, :, COLS:] = spread(away[:, :, COLS:])


def join_pairs_kernel(own_ref, got_ref, keep_ref, *send_refs):
    pair = lax.div(lax.axis_index("batch"), 4)
    for away in range(PAIRS):
        there = lax.bitwise_xor(pair, jnp.int32(away))
        got = got_ref[there].astype(F32)
        total = own_ref[there, :, :COLS] + got[:, :COLS]
        tail = own_ref[there, :, COLS:] + gather_parts(got[:, COLS:])
        if away == 0:
            keep_ref[:, :COLS] = total
            keep_ref[:, COLS:] = tail
        else:
            send_refs[away - 1][:, :COLS] = total.astype(BF16)
            send_refs[away - 1][:, COLS:] = spread(tail)


def feat_sum_kernel(source_ref, feat_out_ref, feat_ref, sems):
    pieces = [pl.ds(first, PROTO // 4) for first in range(0, PROTO, PROTO // 4)]
    fetches = [pltpu.make_async_copy(source_ref.at[at], feat_ref.at[at], sems.at[i]) for i, at in enumerate(pieces)]
    for fetch in fetches:
        fetch.start()
    total = jnp.zeros((16, HALF), F32)
    for fetch, at in zip(fetches, pieces):
        fetch.wait()
        total += jnp.sum(feat_ref[at].astype(F32), axis=0)
    feat_out_ref[:, :HALF] = total[:8]
    feat_out_ref[:, HALF:] = total[8:]


def proto_sum_kernel(keep_ref, first_ref, second_ref, third_ref, after_ref, proto_out_ref, loss_ref):
    total = keep_ref[:, :COLS]
    loss = keep_ref[0:1, COLS : COLS + 1]
    for ref in (first_ref, second_ref, third_ref):
        got = ref[...].astype(F32)
        total += got[:, :COLS]
        loss += gather_parts(got[0:1, COLS:])
    proto_out_ref[...] = total
    loss_ref[...] = loss / CROPS


def per_device(student_feat, teacher_feat, student_proto, teacher_proto):
    swap_cores = [(i, i ^ 1) for i in range(BATCH)]
    swap_pairs = [(i, i ^ 2) for i in range(BATCH)]
    swap_sides = [(i, i ^ SIDE) for i in range(PROTO)]

    def over_batch(array):
        return lax.all_to_all(array, "batch", 0, 0)

    def over_proto(array):
        return lax.all_to_all(array, "proto", 0, 0)

    packed, halved = shape((PROTO, 8, ROWS), BF16), shape((PROTO, 16, HALF), BF16)
    rounded = shape((D, COLS), BF16)
    row_shape = shape((PROTO, ROW_TILES, LANES), BF16)
    first_row_shape = shape((PROTO, ROW_TILES, HALF + LANES), BF16)
    last_shape = shape((PROTO, 5 * ROW_TILES, LANES), BF16)
    col_shape, last_col_shape = shape((BATCH, COL_TILES, LANES), BF16), shape((BATCH, COL_TILES, LANES))
    row_tile, row_part = pltpu.VMEM((ROW_TILES, LANES), F32), pltpu.VMEM((ROWS, LANES), F32)
    col_tile, col_part = pltpu.VMEM((COL_TILES, LANES), F32), pltpu.VMEM((8, COLS), F32)

    (send,) = call(prepare_kernel, [packed], [teacher_feat.T], name="prepare")
    teach = over_proto(send)
    teacher_cols, proto_round, proto_inv = call(
        unit_cols_kernel, [rounded, rounded, shape((1, COLS))], [teacher_proto, student_proto], name="unit_cols"
    )
    teacher_exp, send = call(
        teacher_kernel,
        [pinned((ROWS, COLS)), col_shape],
        [teach, teacher_cols],
        [pltpu.VMEM((ROWS, D), BF16), col_part],
        name="teacher_exp",
    )
    got = over_batch(send)
    (send,) = call(
        first_row_kernel,
        [first_row_shape],
        [pin(teacher_exp), got, student_feat.T],
        [col_tile, row_part, row_tile],
        name="row_pass_1",
    )
    own_half = over_proto(send)
    other_half = lax.ppermute(own_half, "proto", swap_sides)
    (send,) = call(
        col_kernel, [col_shape], [pin(teacher_exp), own_half], [row_part, col_part], name="col_pass_2"
    )
    got = over_batch(send)
    (send,) = call(
        row_kernel,
        [row_shape],
        [pin(teacher_exp), got, other_half],
        [col_tile, row_part, row_tile],
        specs=[VM, VM, ANY],
        name="row_pass_2",
    )
    got = over_proto(send)
    (send,) = call(col_kernel, [last_col_shape], [pin(teacher_exp), got], [row_part, col_part], name="col_pass_3")
    got = over_batch(send)
    student_exp, weighted, raw_feat, feat_round, feat_inv, send = call(
        student_kernel,
        [
            pinned((ROWS, COLS)),
            pinned((ROWS, COLS)),
            shape((D, ROWS), BF16),
            shape((D, ROWS), BF16),
            shape((1, ROWS)),
            last_shape,
        ],
        [own_half, other_half, pin(teacher_exp), proto_round, got],
        [pltpu.VMEM((ROWS, D), BF16), col_tile, row_part, row_part, row_part, row_tile],
        name="student_and_last_row",
    )
    got = over_proto(send)
    half_shape = shape((2, PAIRS, D // BATCH, COLS + LANES))
    split = (PAIRS, 2, 2, D // BATCH)
    order = (2, 2, PAIRS, D // BATCH)
    grad_logit, own, other = call(
        grad_kernel,
        [pinned((ROWS, COLS), BF16), half_shape, half_shape],
        [
            pin(weighted),
            pin(student_exp),
            feat_round.reshape(split + (ROWS,)),
            got,
            stay(student_proto.reshape(split + (COLS,))),
            proto_inv,
        ],
        [
            row_part,
            row_part,
            pltpu.VMEM(order + (ROWS,), BF16),
            pltpu.VMEM(order + (COLS,), BF16),
            pltpu.SemaphoreType.DMA((4,)),
        ],
        specs=[VM] * 4 + [ANY, VM],
        vmem=16,
        name="proto_grad",
    )
    arrived = lax.ppermute(other, "batch", swap_cores)
    feat_part = pl.pallas_call(
        feat_grad_kernel,
        out_shape=halved,
        in_specs=[VM] * 4,
        out_specs=ANY,
        scratch_shapes=[pltpu.VMEM((2, PROTO, 16, QUARTER), BF16), pltpu.SemaphoreType.DMA((2,))],
        compiler_params=pltpu.CompilerParams(vmem_limit_bytes=12 * MIB),
        name="feat_grad",
    )(pin(grad_logit), proto_round, raw_feat, feat_inv)
    pair_shape = (PAIRS, D // BATCH, COLS + LANES)
    keep, send, feat_part = pl.pallas_call(
        join_cores_kernel,
        out_shape=[shape(pair_shape), shape(pair_shape, BF16), halved],
        in_specs=[VM, VM, ANY],
        out_specs=[VM, VM, ANY],
        input_output_aliases={2: 2},
        compiler_params=pltpu.CompilerParams(vmem_limit_bytes=12 * MIB),
        name="join_cores",
    )(own, arrived, feat_part)
    feat_got = over_proto(feat_part)
    arrived = lax.ppermute(send, "batch", swap_pairs)
    block = pair_shape[1:]
    keep, *sends = call(
        join_pairs_kernel,
        [shape(block)] + [shape(block, BF16)] * (PAIRS - 1),
        [keep, arrived],
        flops=LONG,
        name="join_pairs",
    )
    quads = [
        lax.ppermute(send, "batch", [(i, i ^ 4 * away) for i in range(BATCH)])
        for away, send in enumerate(sends, 1)
    ]
    (feat_out,) = call(
        feat_sum_kernel,
        [shape((8, ROWS))],
        [stay(feat_got)],
        [pltpu.VMEM((PROTO, 16, HALF), BF16), pltpu.SemaphoreType.DMA((4,))],
        specs=[ANY],
        name="feat_sum",
    )
    proto_out, loss = call(
        proto_sum_kernel,
        [shape((D // BATCH, COLS)), shape((1, 1))],
        [keep, *quads, feat_out],
        specs=[VM] * 4 + [ANY],
        name="proto_sum",
    )
    return (loss.reshape(()), feat_out.T, proto_out)


def solution(mesh):
    placed = (P("batch", "proto"), P("batch", "proto"), P(None, "proto"), P(None, "proto"))
    return jax.shard_map(
        per_device,
        mesh=mesh,
        in_specs=placed,
        out_specs=(P(), P("batch", "proto"), P("batch", "proto")),
        check_vma=False,
    )
```

```python
import jax
import jax.numpy as jnp
from jax import lax
from jax.experimental import pallas as pl
from jax.experimental.pallas import tpu as pltpu
from jax.sharding import PartitionSpec as P

F32, BF16 = jnp.float32, jnp.bfloat16
SWEEPS = 3
LOG2E = 1.4426950408889634
STUDENT_SCALE = LOG2E / 0.1
TEACHER_SCALE = LOG2E / 0.07
D, ROWS, COLS = 256, 1024, 2048
LANES = 128
ROW_TILES, COL_TILES = ROWS // LANES, COLS // LANES
PROTO, BATCH = 32, 16
PAIRS = BATCH // 4
SIDE = 8
CROPS, PROTOS = ROWS * BATCH, COLS * PROTO
HALF = ROWS // 2
QUARTER = ROWS // 4
CHUNK = 512
BAND = 32
MIB = 1024 * 1024
LONG = 200_000_000_000

VM = pl.BlockSpec(memory_space=pltpu.VMEM)
ANY = pl.BlockSpec(memory_space=pl.ANY)


def shape(dims, dtype=F32):
    return jax.ShapeDtypeStruct(dims, dtype)


def pinned(dims, dtype=F32):
    return pltpu.VMEM(dims, dtype)


def pin(array):
    return pltpu.with_memory_space_constraint(array, pltpu.VMEM)


def stay(array):
    return pltpu.with_memory_space_constraint(array, pltpu.HBM)


def call(body, outs, args, scratch=(), specs=None, name=None, vmem=12, aliases=None, flops=None):
    return pl.pallas_call(
        body,
        out_shape=outs,
        in_specs=specs or [VM] * len(args),
        out_specs=[VM] * len(outs),
        scratch_shapes=list(scratch),
        compiler_params=pltpu.CompilerParams(vmem_limit_bytes=vmem * MIB),
        input_output_aliases=aliases or {},
        cost_estimate=flops and pl.CostEstimate(flops=flops, bytes_accessed=0, transcendentals=0),
        name=name,
    )(*args)


def lane_major(partial_ref, out_ref):
    for j in range(ROW_TILES):
        tile = partial_ref[LANES * j : LANES * (j + 1), :]
        out_ref[j : j + 1, :] = jnp.sum(tile.T, axis=0, keepdims=True)


def sublane_major(values, out_ref):
    for j in range(ROW_TILES):
        out_ref[LANES * j : LANES * (j + 1), :] = jnp.broadcast_to(values[j : j + 1, :], (LANES, LANES)).T


def prepare_kernel(teach_ref, teach_out):
    put(teach_out, teach_ref[...])


def unit_cols_kernel(teacher_ref, student_ref, teacher_out, student_out, inv_ref):
    for lo in range(0, COLS, CHUNK):
        lanes = slice(lo, lo + CHUNK)
        teacher_out[:, lanes] = unit_rows(teacher_ref[:, lanes].astype(F32)).astype(BF16)
        x = student_ref[:, lanes].astype(F32)
        inv = lax.rsqrt(jnp.sum(x * x, axis=0, keepdims=True) + 1e-06)
        inv_ref[:, lanes] = inv
        student_out[:, lanes] = (x * inv).astype(BF16)


def unit_rows(x):
    return x * lax.rsqrt(jnp.sum(x * x, axis=0, keepdims=True) + 1e-06)


def put(out_ref, value, rows=slice(None), lanes=slice(None)):
    for peer in range(out_ref.shape[0]):
        out_ref[peer, rows, lanes] = value


def col_rows(acc_ref):
    total = jnp.sum(acc_ref[...], axis=0, keepdims=True)
    return jnp.concatenate([total[:, LANES * i : LANES * (i + 1)] for i in range(COL_TILES)], axis=0)


def row_block(j):
    return pl.ds(pl.multiple_of(j * LANES, LANES), LANES)


def teacher_kernel(feat_ref, cols_ref, exp_ref, out_ref, rows_ref, acc_ref):
    for half in range(2):
        lanes = slice(HALF * half, HALF * (half + 1))
        x = feat_ref[:, :, lanes].astype(F32).reshape(D, HALF)
        rows_ref[lanes, :] = unit_rows(x).T.astype(BF16)
    for lo in range(0, COLS, CHUNK):
        lanes = slice(lo, lo + CHUNK)
        z = jnp.dot(rows_ref[...], cols_ref[:, lanes], preferred_element_type=F32)
        e = jnp.exp2(z * TEACHER_SCALE)
        exp_ref[:, lanes] = e
        acc_ref[:, lanes] = jnp.sum(e.reshape(ROWS // 8, 8, CHUNK), axis=0)
    put(out_ref, col_rows(acc_ref).astype(out_ref.dtype))


def col_scale_of(got_ref):
    return 1.0 / (PROTOS * jnp.sum(got_ref[...].astype(F32), axis=0))


def row_sums(exp_ref, scale_ref, part_ref, sum_ref):
    def block(pair, carry):
        for j in (2 * pair, 2 * pair + 1):
            at = row_block(j)
            acc = jnp.zeros((LANES, LANES), F32)
            for i in range(COL_TILES):
                acc += exp_ref[at, LANES * i : LANES * (i + 1)] * scale_ref[i : i + 1, :]
            part_ref[at, :] = acc
        return carry

    lax.fori_loop(0, ROW_TILES // 2, block, 0)
    lane_major(part_ref, sum_ref)


def first_row_kernel(exp_ref, got_ref, stud_ref, out_ref, scale_ref, part_ref, sum_ref):
    scale_ref[...] = col_scale_of(got_ref)
    row_sums(exp_ref, scale_ref, part_ref, sum_ref)
    sums = sum_ref[...].astype(BF16)
    for peer in range(PROTO):
        half = peer // SIDE % 2
        out_ref[peer, :, :HALF] = stud_ref[:, HALF * half : HALF * (half + 1)]
        out_ref[peer, :, HALF:] = sums


def row_kernel(exp_ref, got_ref, after_ref, out_ref, scale_ref, part_ref, sum_ref):
    scale_ref[...] = col_scale_of(got_ref)
    row_sums(exp_ref, scale_ref, part_ref, sum_ref)
    put(out_ref, sum_ref[...].astype(BF16))


def col_kernel(exp_ref, got_ref, out_ref, rows_ref, acc_ref):
    sublane_major(1.0 / (CROPS * jnp.sum(got_ref[:, :, -LANES:].astype(F32), axis=0)), rows_ref)
    acc_ref[...] = jnp.zeros_like(acc_ref)

    def block(pair, carry):
        for j in (2 * pair, 2 * pair + 1):
            at = row_block(j)
            r = rows_ref[at, :]
            for i in range(COL_TILES):
                lanes = slice(LANES * i, LANES * (i + 1))
                acc_ref[:, lanes] += jnp.sum((exp_ref[at, lanes] * r).reshape(LANES // 8, 8, LANES), axis=0)
        return carry

    lax.fori_loop(0, ROW_TILES // 2, block, 0)
    put(out_ref, col_rows(acc_ref).astype(out_ref.dtype))


def student_kernel(
    own_ref, other_ref, teacher_ref, cols_ref, got_ref, exp_ref, weighted_ref, raw_feat_ref, feat_out_ref, feat_inv_ref,
    out_ref, rows_ref, scale_ref, part_ref, cross_ref, total_ref, sum_ref,
):
    scale_ref[...] = col_scale_of(got_ref)
    side = lax.rem(lax.div(lax.axis_index("proto"), SIDE), 2)
    for half in range(2):
        lanes = slice(HALF * half, HALF * (half + 1))
        own, other = own_ref[:, :, :HALF].astype(F32), other_ref[:, :, :HALF].astype(F32)
        x = jnp.where(side == half, own, other).reshape(D, HALF)
        raw_feat_ref[:, lanes] = x.astype(BF16)
        inv = lax.rsqrt(jnp.sum(x * x, axis=0, keepdims=True) + 1e-06)
        unit = x * inv
        rows_ref[lanes, :] = unit.T.astype(BF16)
        feat_out_ref[:, lanes] = unit.astype(BF16)
        feat_inv_ref[:, lanes] = inv

    for lo in range(0, COLS, CHUNK):
        z = jnp.dot(rows_ref[...], cols_ref[:, lo : lo + CHUNK], preferred_element_type=F32)
        for top in range(0, ROWS, BAND):
            band = slice(top, top + BAND)
            if lo == 0:
                acc = cross = total = jnp.zeros((BAND, LANES), F32)
            else:
                acc, cross, total = part_ref[band, :], cross_ref[band, :], total_ref[band, :]
            for i in range(lo // LANES, (lo + CHUNK) // LANES):
                lanes = slice(LANES * i, LANES * (i + 1))
                logit = z[band, LANES * i - lo : LANES * (i + 1) - lo]
                e = jnp.exp2(logit * STUDENT_SCALE)
                exp_ref[band, lanes] = e
                weighted = teacher_ref[band, lanes] * scale_ref[i : i + 1, :]
                weighted_ref[band, lanes] = weighted
                acc += weighted
                cross += weighted * logit
                total += e
            part_ref[band, :], cross_ref[band, :], total_ref[band, :] = acc, cross, total
    refs = (part_ref, total_ref, cross_ref)
    for i, ref in enumerate(refs):
        lane_major(ref, sum_ref.at[pl.ds(ROW_TILES * i, ROW_TILES)])
    sends = []
    for i in range(len(refs)):
        sums = sum_ref[ROW_TILES * i : ROW_TILES * (i + 1), :]
        high = sums.astype(BF16).astype(F32)
        sends += [high, sums - high]
    put(out_ref, jnp.concatenate(sends[:5], axis=0).astype(BF16))


def grad_kernel(
    weighted_ref, exp_ref, feat_ref, got_ref, source_ref, cols_inv_ref,
    grad_ref, own_ref, other_ref, target_ref, soft_ref, order_ref, raw_cols_ref, sems,
):
    batch = lax.axis_index("batch")
    core, odd = lax.rem(batch, 2), lax.rem(lax.div(batch, 2), 2)
    fetches = []
    for away in range(2):
        parity = odd if away == 0 else 1 - odd
        for side in range(2):
            other = core if side == 0 else 1 - core
            fetches.append(
                pltpu.make_async_copy(source_ref.at[:, parity, other], raw_cols_ref.at[side, away], sems.at[len(fetches)])
            )
            for pair in range(PAIRS):
                order_ref[side, away, pair] = feat_ref[pair, parity, other]
    for fetch in fetches:
        fetch.start()
    got = jnp.sum(got_ref[...].astype(F32), axis=0).reshape(5, ROW_TILES, LANES)
    sums, totals, cross = got[0] + got[1], got[2] + got[3], got[4] / 0.1
    local_loss = jnp.sum(jnp.log(totals) - cross / sums)
    sublane_major(PROTOS / sums, target_ref)
    sublane_major(PROTOS / totals, soft_ref)

    def block(j, carry):
        at = pl.ds(pl.multiple_of(j * 64, 64), 64)
        target_rows, soft_rows = target_ref[at, :], soft_ref[at, :]
        for i in range(COL_TILES):
            lanes = slice(LANES * i, LANES * (i + 1))
            grad_ref[at, lanes] = (exp_ref[at, lanes] * soft_rows - weighted_ref[at, lanes] * target_rows).astype(BF16)
        return carry

    lax.fori_loop(0, ROWS // 64, block, 0)

    for fetch in fetches:
        fetch.wait()
    half_block = (2, PAIRS, D // BATCH, CHUNK)
    for lo in range(0, COLS, CHUNK):
        lanes = slice(lo, lo + CHUNK)
        rows = order_ref[...].reshape(D, ROWS)
        part = jnp.dot(rows, grad_ref[:, lanes], preferred_element_type=F32)
        unit = raw_cols_ref[:, :, :, :, lanes].astype(F32).reshape(D, CHUNK) * cols_inv_ref[:, lanes]
        part = part - unit * jnp.sum(unit * part, axis=0, keepdims=True)
        own_ref[:, :, :, lanes] = part[: D // 2].reshape(half_block)
        other_ref[:, :, :, lanes] = part[D // 2 :].reshape(half_block)
    loss_row = jnp.full((2, PAIRS, D // BATCH, LANES), local_loss, F32)
    own_ref[:, :, :, COLS:] = loss_row
    other_ref[:, :, :, COLS:] = loss_row


def feat_grad_kernel(grad_ref, cols_ref, raw_feat_ref, feat_inv_ref, out_ref, stage_ref, sems):
    copies = []
    for side in range(2):
        parts = []
        for half in range(2):
            lanes = slice(HALF * half + QUARTER * side, HALF * half + QUARTER * (side + 1))
            part = lax.dot_general(
                cols_ref[...], grad_ref[lanes, :], (((1,), (1,)), ((), ())), preferred_element_type=F32
            )
            unit = raw_feat_ref[:, lanes].astype(F32) * feat_inv_ref[:, lanes]
            part = part - unit * jnp.sum(unit * part, axis=0, keepdims=True)
            parts.append(part.reshape(PROTO, 8, QUARTER))
        stage_ref[side] = jnp.concatenate(parts, axis=1).astype(BF16)
        there = out_ref.at[:, :, pl.ds(QUARTER * side, QUARTER)]
        copies.append(pltpu.make_async_copy(stage_ref.at[side], there, sems.at[side]))
        copies[-1].start()
    for copy in copies:
        copy.wait()


def spread(tail):
    lane = lax.broadcasted_iota(jnp.int32, tail.shape, tail.ndim - 1)
    high = tail.astype(BF16).astype(F32)
    middle = (tail - high).astype(BF16).astype(F32)
    return jnp.where(lane == 0, high, jnp.where(lane == 1, middle, tail - high - middle)).astype(BF16)


def gather_parts(tail):
    return tail[..., 0:1] + tail[..., 1:2] + tail[..., 2:3]


def join_cores_kernel(own_ref, got_ref, feat_ref, keep_ref, send_ref, feat_out_ref):
    keep_ref[...] = own_ref[0] + got_ref[0]
    away = own_ref[1] + got_ref[1]
    send_ref[:, :, :COLS] = away[:, :, :COLS].astype(BF16)
    send_ref[:, :, COLS:] = spread(away[:, :, COLS:])


def join_pairs_kernel(own_ref, got_ref, keep_ref, *send_refs):
    pair = lax.div(lax.axis_index("batch"), 4)
    for away in range(PAIRS):
        there = lax.bitwise_xor(pair, jnp.int32(away))
        got = got_ref[there].astype(F32)
        total = own_ref[there, :, :COLS] + got[:, :COLS]
        tail = own_ref[there, :, COLS:] + gather_parts(got[:, COLS:])
        if away == 0:
            keep_ref[:, :COLS] = total
            keep_ref[:, COLS:] = tail
        else:
            send_refs[away - 1][:, :COLS] = total.astype(BF16)
            send_refs[away - 1][:, COLS:] = spread(tail)


def feat_sum_kernel(source_ref, feat_out_ref, feat_ref, sems):
    pieces = [pl.ds(first, PROTO // 4) for first in range(0, PROTO, PROTO // 4)]
    fetches = [pltpu.make_async_copy(source_ref.at[at], feat_ref.at[at], sems.at[i]) for i, at in enumerate(pieces)]
    for fetch in fetches:
        fetch.start()
    total = jnp.zeros((16, HALF), F32)
    for fetch, at in zip(fetches, pieces):
        fetch.wait()
        total += jnp.sum(feat_ref[at].astype(F32), axis=0)
    feat_out_ref[:, :HALF] = total[:8]
    feat_out_ref[:, HALF:] = total[8:]


def proto_sum_kernel(keep_ref, first_ref, second_ref, third_ref, after_ref, proto_out_ref, loss_ref):
    total = keep_ref[:, :COLS]
    loss = keep_ref[0:1, COLS : COLS + 1]
    for ref in (first_ref, second_ref, third_ref):
        got = ref[...].astype(F32)
        total += got[:, :COLS]
        loss += gather_parts(got[0:1, COLS:])
    proto_out_ref[...] = total
    loss_ref[...] = loss / CROPS


def per_device(student_feat, teacher_feat, student_proto, teacher_proto):
    swap_cores = [(i, i ^ 1) for i in range(BATCH)]
    swap_pairs = [(i, i ^ 2) for i in range(BATCH)]
    swap_sides = [(i, i ^ SIDE) for i in range(PROTO)]

    def over_batch(array):
        return lax.all_to_all(array, "batch", 0, 0)

    def over_proto(array):
        return lax.all_to_all(array, "proto", 0, 0)

    packed, halved = shape((PROTO, 8, ROWS), BF16), shape((PROTO, 16, HALF), BF16)
    rounded = shape((D, COLS), BF16)
    row_shape = shape((PROTO, ROW_TILES, LANES), BF16)
    first_row_shape = shape((PROTO, ROW_TILES, HALF + LANES), BF16)
    last_shape = shape((PROTO, 5 * ROW_TILES, LANES), BF16)
    col_shape, last_col_shape = shape((BATCH, COL_TILES, LANES), BF16), shape((BATCH, COL_TILES, LANES))
    row_tile, row_part = pltpu.VMEM((ROW_TILES, LANES), F32), pltpu.VMEM((ROWS, LANES), F32)
    col_tile, col_part = pltpu.VMEM((COL_TILES, LANES), F32), pltpu.VMEM((8, COLS), F32)

    (send,) = call(prepare_kernel, [packed], [teacher_feat.T], name="prepare")
    teach = over_proto(send)
    teacher_cols, proto_round, proto_inv = call(
        unit_cols_kernel, [rounded, rounded, shape((1, COLS))], [teacher_proto, student_proto], name="unit_cols"
    )
    teacher_exp, send = call(
        teacher_kernel,
        [pinned((ROWS, COLS)), col_shape],
        [teach, teacher_cols],
        [pltpu.VMEM((ROWS, D), BF16), col_part],
        name="teacher_exp",
    )
    got = over_batch(send)
    (send,) = call(
        first_row_kernel,
        [first_row_shape],
        [pin(teacher_exp), got, student_feat.T],
        [col_tile, row_part, row_tile],
        name="row_pass_1",
    )
    own_half = over_proto(send)
    other_half = lax.ppermute(own_half, "proto", swap_sides)
    (send,) = call(
        col_kernel, [col_shape], [pin(teacher_exp), own_half], [row_part, col_part], name="col_pass_2"
    )
    got = over_batch(send)
    (send,) = call(
        row_kernel,
        [row_shape],
        [pin(teacher_exp), got, other_half],
        [col_tile, row_part, row_tile],
        specs=[VM, VM, ANY],
        name="row_pass_2",
    )
    got = over_proto(send)
    (send,) = call(col_kernel, [last_col_shape], [pin(teacher_exp), got], [row_part, col_part], name="col_pass_3")
    got = over_batch(send)
    student_exp, weighted, raw_feat, feat_round, feat_inv, send = call(
        student_kernel,
        [
            pinned((ROWS, COLS)),
            pinned((ROWS, COLS)),
            shape((D, ROWS), BF16),
            shape((D, ROWS), BF16),
            shape((1, ROWS)),
            last_shape,
        ],
        [own_half, other_half, pin(teacher_exp), proto_round, got],
        [pltpu.VMEM((ROWS, D), BF16), col_tile, row_part, row_part, row_part, pltpu.VMEM((3 * ROW_TILES, LANES), F32)],
        name="student_and_last_row",
    )
    got = over_proto(send)
    half_shape = shape((2, PAIRS, D // BATCH, COLS + LANES))
    split = (PAIRS, 2, 2, D // BATCH)
    order = (2, 2, PAIRS, D // BATCH)
    grad_logit, own, other = call(
        grad_kernel,
        [pinned((ROWS, COLS), BF16), half_shape, half_shape],
        [
            pin(weighted),
            pin(student_exp),
            feat_round.reshape(split + (ROWS,)),
            got,
            stay(student_proto.reshape(split + (COLS,))),
            proto_inv,
        ],
        [
            row_part,
            row_part,
            pltpu.VMEM(order + (ROWS,), BF16),
            pltpu.VMEM(order + (COLS,), BF16),
            pltpu.SemaphoreType.DMA((4,)),
        ],
        specs=[VM] * 4 + [ANY, VM],
        vmem=16,
        name="proto_grad",
    )
    arrived = lax.ppermute(other, "batch", swap_cores)
    feat_part = pl.pallas_call(
        feat_grad_kernel,
        out_shape=halved,
        in_specs=[VM] * 4,
        out_specs=ANY,
        scratch_shapes=[pltpu.VMEM((2, PROTO, 16, QUARTER), BF16), pltpu.SemaphoreType.DMA((2,))],
        compiler_params=pltpu.CompilerParams(vmem_limit_bytes=12 * MIB),
        name="feat_grad",
    )(pin(grad_logit), proto_round, raw_feat, feat_inv)
    pair_shape = (PAIRS, D // BATCH, COLS + LANES)
    keep, send, feat_part = pl.pallas_call(
        join_cores_kernel,
        out_shape=[shape(pair_shape), shape(pair_shape, BF16), halved],
        in_specs=[VM, VM, ANY],
        out_specs=[VM, VM, ANY],
        input_output_aliases={2: 2},
        compiler_params=pltpu.CompilerParams(vmem_limit_bytes=12 * MIB),
        name="join_cores",
    )(own, arrived, feat_part)
    feat_got = over_proto(feat_part)
    arrived = lax.ppermute(send, "batch", swap_pairs)
    block = pair_shape[1:]
    keep, *sends = call(
        join_pairs_kernel,
        [shape(block)] + [shape(block, BF16)] * (PAIRS - 1),
        [keep, arrived],
        flops=LONG,
        name="join_pairs",
    )
    quads = [
        lax.ppermute(sends[away - 1], "batch", [(i, i ^ 4 * away) for i in range(BATCH)]) for away in (2, 3, 1)
    ]
    (feat_out,) = call(
        feat_sum_kernel,
        [shape((8, ROWS))],
        [stay(feat_got)],
        [pltpu.VMEM((PROTO, 16, HALF), BF16), pltpu.SemaphoreType.DMA((4,))],
        specs=[ANY],
        name="feat_sum",
    )
    proto_out, loss = call(
        proto_sum_kernel,
        [shape((D // BATCH, COLS)), shape((1, 1))],
        [keep, *quads, feat_out],
        specs=[VM] * 4 + [ANY],
        name="proto_sum",
    )
    return (loss.reshape(()), feat_out.T, proto_out)


def solution(mesh):
    placed = (P("batch", "proto"), P("batch", "proto"), P(None, "proto"), P(None, "proto"))
    return jax.shard_map(
        per_device,
        mesh=mesh,
        in_specs=placed,
        out_specs=(P(), P("batch", "proto"), P("batch", "proto")),
        check_vma=False,
    )
```
